512 devices in a mesh: space: 128 (over x, y_hi, z), tm: 4 (over y_lo, core).
Axes of the slice: x: 4, y: 4 (y_hi: 2, y_lo: 2; y = y_hi * 2 + y_lo), z: 16, core: 2. Of those that a mesh axis runs over, the one named last changes fastest.
Arguments:
- source_field: float32 [2, 4, 3, 1048576], P(None, None, None, ('tm', 'space')), may hold values from -6 to 6
- initial_guess: float32 [2, 4, 3, 1048576], P(None, None, None, ('tm', 'space')), may hold values from -1.8 to 1.8
- gauge_links: bfloat16 [4, 2, 3, 3, 1048576], P(None, None, None, None, ('tm', 'space')), may hold values from -0.8984375 to 0.8984375
- clover: bfloat16 [2, 2, 6, 6, 1048576], P(None, None, None, None, ('tm', 'space')), may hold values from -1.5 to 8.5
- boundary_signs: int32 [65536], P('space'), may hold values from 0 to 1
- null_vectors: bfloat16 [24, 2, 4, 3, 1048576], P(None, None, None, None, ('tm', 'space')), may hold values from -0.29882812 to 0.29882812
- coarse_ops: bfloat16 [9, 2, 24, 98304], P(None, None, None, ('tm', 'space')), may hold values from -0.41992188 to 0.41992188
Outputs:
- smoothed: float32 [2, 4, 3, 1048576], P(None, None, None, ('tm', 'space'))
- coarse_out: float32 [2, 24, 4096], P(None, None, ('tm', 'space'))
The draws below stay inside these ranges and needn't reach their ends.
All inputs are finite; a program needn't handle non-finite values.
Results may differ from the reference program's by a relative error of at most 0.0029.
Values sent between devices are 32-bit elements; how exact they have to be, the bound alone decides.
A program may use at most 128 MiB of HBM per device.

```python
import jax
import jax.numpy as jnp
import numpy as np
from jax import lax

NV = 24
AGG = 4
TILE = 8
TILES_Y = 4
TILES_Z = 8
SITES = 65536
NT = 16
VOL = 1048576
AGGS = 1024
CAGGS = 4096
N_SPACE = 128
N_TM = 4


def draw_clover(key, part):
    key = jax.random.fold_in(key, 7)
    noise_key, diagonal_key = jax.random.split(key)
    extent = (2, 2, 6, 6, VOL)
    noise_values = jnp.clip(jax.random.normal(noise_key, extent, jnp.float32), -5.0, 5.0) * 0.3
    diagonal_shift = 5.0 + 2.0 * jax.random.uniform(diagonal_key, (2, 6, VOL), jnp.float32)
    identity = jnp.eye(6, dtype=jnp.float32)[:, :, None]
    real_part = noise_values[:, 0] + identity * diagonal_shift[:, :, None]
    return jnp.stack([real_part, noise_values[:, 1]], axis=1).astype(jnp.bfloat16)


def set_ends(values, key, low, largest):
    longest = values.shape.index(max(values.shape))
    spots = []
    for shift in (0, 1):
        where = [jax.random.randint(jax.random.fold_in(key, axis), (), 0, length) for axis, length in enumerate(values.shape)]
        where[longest] = (where[longest] + shift) % values.shape[longest]
        spots.append(tuple(where))
    return values.at[spots[0]].set(low).at[spots[1]].set(largest)


def block_scale(rng, shape, shards, least, largest):
    loudness, own = 1.0, jax.random.fold_in(rng, 6)
    for dim, blocks in shards:
        steps = jnp.exp(jax.random.uniform(jax.random.fold_in(own, dim), (blocks,), jnp.float32, least / len(shards), largest / len(shards)))
        loudness = loudness * jnp.repeat(steps, shape[dim] // blocks).reshape([-1 if axis == dim else 1 for axis in range(len(shape))])
    return loudness


def normal_values(own_key, dims, spread, most, shards=(), kind=jnp.bfloat16):
    array = spread * jax.random.normal(own_key, dims, jnp.float32)
    if shards:
        array = array * block_scale(own_key, dims, shards, -0.22, 0.18)
    return jnp.clip(array, -most, most).astype(kind)


def setup_inputs(seed: int = 0) -> dict:
    key_of = jax.random.split(jax.random.key(seed), 8)
    return {
        "source_field": normal_values(key_of[0], (2, 4, 3, VOL), 1.0, 6.0, ((3, 512),), jnp.float32),
        "initial_guess": normal_values(key_of[1], (2, 4, 3, VOL), 0.3, 1.8, ((3, 512),), jnp.float32),
        "gauge_links": normal_values(key_of[2], (4, 2, 3, 3, VOL), 0.15, 0.8984375, ((4, 512),)),
        "clover": draw_clover(jax.random.fold_in(key_of[7], 71), 0),
        "boundary_signs": set_ends(jax.random.randint(key_of[4], (SITES,), 0, 2), jax.random.fold_in(key_of[4], 1), 0, 1).astype(jnp.int32),
        "null_vectors": normal_values(key_of[5], (NV, 2, 4, 3, VOL), 0.05, 0.29882812, ((4, 512),)),
        "coarse_ops": normal_values(key_of[6], (9, 2, NV, CAGGS * NV), 0.07, 0.41992188, ((3, 512),)),
    }


relaxation = 0.16


def spin_blocks():
    block_re = np.zeros((4, 2, 2), np.float32)
    block_im = np.zeros((4, 2, 2), np.float32)
    block_im[0] = [[0.0, -1.0], [-1.0, 0.0]]
    block_re[1] = [[0.0, -1.0], [1.0, 0.0]]
    block_im[2] = [[-1.0, 0.0], [0.0, 1.0]]
    block_re[3] = [[1.0, 0.0], [0.0, 1.0]]
    return block_re, block_im


def projector(direction, parity):
    block_re, block_im = spin_blocks()
    gamma_re = np.zeros((4, 4), np.float32)
    gamma_im = np.zeros((4, 4), np.float32)
    gamma_re[:2, 2:] = block_re[direction]
    gamma_im[:2, 2:] = block_im[direction]
    gamma_re[2:, :2] = block_re[direction].T
    gamma_im[2:, :2] = -block_im[direction].T
    return np.eye(4, dtype=np.float32) + parity * gamma_re, parity * gamma_im


def spin_mix(matrix_re, matrix_im, spinor):
    spinor_re, spinor_im = spinor[0], spinor[1]
    rows_re, rows_im = [], []
    for out_spin in range(matrix_re.shape[0]):
        total_re = jnp.zeros_like(spinor_re[0])
        total_im = jnp.zeros_like(spinor_im[0])
        for in_spin in range(matrix_re.shape[1]):
            factor_re = float(matrix_re[out_spin, in_spin])
            factor_im = float(matrix_im[out_spin, in_spin])
            if factor_re != 0.0:
                total_re = total_re + factor_re * spinor_re[in_spin]
                total_im = total_im + factor_re * spinor_im[in_spin]
            if factor_im != 0.0:
                total_re = total_re - factor_im * spinor_im[in_spin]
                total_im = total_im + factor_im * spinor_re[in_spin]
        rows_re.append(total_re)
        rows_im.append(total_im)
    return jnp.stack([jnp.stack(rows_re), jnp.stack(rows_im)])


def color_apply(gauge_link, spinor, dagger):
    link_re, link_im = gauge_link[0], gauge_link[1]
    if dagger:
        link_re = jnp.swapaxes(link_re, 0, 1)
        link_im = -jnp.swapaxes(link_im, 0, 1)
    spinor_re = spinor[0][:, None]
    spinor_im = spinor[1][:, None]
    result_re = jnp.sum(link_re[None] * spinor_re - link_im[None] * spinor_im, axis=2)
    result_im = jnp.sum(link_re[None] * spinor_im + link_im[None] * spinor_re, axis=2)
    return jnp.stack([result_re, result_im])


def clover_apply(clover, spinor):
    extent = spinor.shape
    blocks = spinor.reshape((2, 2, 6) + extent[3:])
    clover_re = clover[:, 0].astype(jnp.float32)
    clover_im = clover[:, 1].astype(jnp.float32)
    blocks_re = blocks[0][:, None]
    blocks_im = blocks[1][:, None]
    result_re = jnp.sum(clover_re * blocks_re - clover_im * blocks_im, axis=2)
    result_im = jnp.sum(clover_re * blocks_im + clover_im * blocks_re, axis=2)
    return jnp.stack([result_re, result_im]).reshape(extent)


def to_lattice(values):
    leading = values.shape[:-1]
    view = values.reshape(leading + (N_TM, N_SPACE, AGG, TILE ** 3))
    return jnp.swapaxes(view, -3, -2).reshape(leading + (NT, SITES))


def from_lattice(values):
    leading = values.shape[:-2]
    view = values.reshape(leading + (N_TM, AGG, N_SPACE, TILE ** 3))
    return jnp.swapaxes(view, -3, -2).reshape(leading + (VOL,))


def lattice_move(values, direction, offset, side_len):
    if direction == 3:
        return jnp.roll(values, offset, axis=-2)
    leading = values.shape[:-1]
    view = values.reshape(leading + (N_SPACE, side_len, side_len, side_len))
    stride = (TILES_Y * TILES_Z, TILES_Z, 1)[direction]
    inner = jnp.roll(view, offset, axis=-1 - direction)
    crossed = jnp.roll(inner, offset * stride, axis=-4)
    edge = 0 if offset > 0 else side_len - 1
    position = lax.broadcasted_iota(jnp.int32, (side_len, side_len, side_len), 2 - direction)
    chosen = jnp.where(position == edge, crossed, inner)
    return chosen.reshape(values.shape)


def dirac_apply(spinor, links_full, clover):
    hops = jnp.zeros_like(spinor)
    for direction in range(4):
        minus_re, minus_im = projector(direction, -1.0)
        plus_re, plus_im = projector(direction, 1.0)
        ahead_term = color_apply(links_full[direction], spin_mix(minus_re, minus_im, lattice_move(spinor, direction, -1, TILE)), False)
        behind_link = lattice_move(links_full[direction], direction, 1, TILE)
        behind = color_apply(behind_link, spin_mix(plus_re, plus_im, lattice_move(spinor, direction, 1, TILE)), True)
        hops = hops + ahead_term + behind
    return clover_apply(clover, spinor) - 0.5 * hops


def restrict(null_vectors, lowered):
    stacked = jnp.stack([jnp.stack([lowered[0], lowered[1]]), jnp.stack([lowered[1], -lowered[0]])])
    extent = null_vectors.shape
    time_blocks = extent[4] // AGG
    tile_count = extent[5] // TILE ** 3
    side_len = TILE // AGG
    blocked = (time_blocks, AGG, tile_count, side_len, AGG, side_len, AGG, side_len, AGG)
    vectors = null_vectors.reshape(extent[:4] + blocked).astype(jnp.float32)
    lowers = stacked.reshape((2, 2, 4, 3) + blocked).astype(jnp.float32)
    result = jnp.einsum("kcsqtunzwyvxh,ocsqtunzwyvxh->oktnzyx", vectors, lowers, preferred_element_type=jnp.float32)
    return result.reshape((2, extent[0], time_blocks, tile_count * side_len ** 3))


def coarse_apply(operators, neighbors):
    total_re = jnp.zeros(neighbors[0][0].shape, jnp.float32)
    total_im = jnp.zeros(neighbors[0][0].shape, jnp.float32)
    for offset in range(9):
        vector_re = neighbors[offset][0][None]
        vector_im = neighbors[offset][1][None]
        oper_re = operators[offset, 0]
        oper_im = operators[offset, 1]
        total_re = total_re + jnp.sum(oper_re * vector_re - oper_im * vector_im, axis=1)
        total_im = total_im + jnp.sum(oper_re * vector_im + oper_im * vector_re, axis=1)
    return jnp.stack([total_re, total_im])


def reference(source_field, initial_guess, gauge_links, clover, boundary_signs, null_vectors, coarse_ops):
    source_lat = to_lattice(source_field)
    clover_lat = to_lattice(clover)
    sign_values = (2 * boundary_signs - 1).astype(jnp.float32)
    links_full = to_lattice(gauge_links).astype(jnp.float32)
    time_factor = jnp.concatenate([jnp.ones((NT - 1, SITES), jnp.float32), sign_values.reshape(1, SITES)], axis=0)
    links_full = jnp.concatenate([links_full[:3], (links_full[3] * time_factor)[None]], axis=0)
    spinor = to_lattice(initial_guess)
    for sweep_index in range(2):
        spinor = spinor + relaxation * (source_lat - dirac_apply(spinor, links_full, clover_lat))
    residual = source_lat - dirac_apply(spinor, links_full, clover_lat)
    coarse_in = restrict(to_lattice(null_vectors), residual.astype(jnp.bfloat16))
    side_len = TILE // AGG
    neighbors = [coarse_in]
    for direction in range(4):
        for offset in (-1, 1):
            neighbors.append(lattice_move(coarse_in, direction, offset, side_len))
    operators = coarse_ops.astype(jnp.float32).reshape((9, 2, NV, N_TM, AGGS, NV))
    operators = jnp.transpose(operators, (0, 1, 2, 5, 3, 4))
    coarse_out = coarse_apply(operators, neighbors)
    return from_lattice(spinor), coarse_out.reshape((2, NV, CAGGS))
```

```python
import jax
import jax.numpy as jnp
from jax import lax
from jax.experimental import pallas as pl
from jax.experimental.pallas import tpu as pltpu
from jax.sharding import PartitionSpec as P

F32 = jnp.float32
BF16 = jnp.bfloat16
NV = 24
STRIDES = (32, 8, 1)
SPIN = (
    ((3, "-i"), (2, "-i")),
    ((3, "-1"), (2, "+1")),
    ((2, "-i"), (3, "+i")),
    ((2, "+1"), (3, "+1")),
)
CONJ = {"+1": "+1", "-1": "-1", "+i": "-i", "-i": "+i"}
NEG = {"+1": "-1", "-1": "+1", "+i": "-i", "-i": "+i"}
PAD = 8


def add_phase(acc, x, phase):
    if phase == "+1":
        return acc[0] + x[0], acc[1] + x[1]
    if phase == "-1":
        return acc[0] - x[0], acc[1] - x[1]
    if phase == "+i":
        return acc[0] - x[1], acc[1] + x[0]
    return acc[0] + x[1], acc[1] - x[0]


def lane_roll(x, shift):
    shift = shift % 128
    return x if shift == 0 else pltpu.roll(x, shift, 1)


def row_roll(x, shift):
    shift = shift % 8
    return x if shift == 0 else pltpu.roll(x, shift, 0)


def spinor_rows(p, s, c, v):
    return pl.ds(((p * 3 + c) * 16 + 8 * v) * 4 + s, 8, stride=4)


def mul_add(acc, a, b, conj):
    if conj:
        re, im = a[0] * b[0] + a[1] * b[1], a[0] * b[1] - a[1] * b[0]
    else:
        re, im = a[0] * b[0] - a[1] * b[1], a[0] * b[1] + a[1] * b[0]
    return (re, im) if acc is None else (acc[0] + re, acc[1] + im)


def kernel(
    n_space, n_tm,
    src_hbm, guess_hbm, gauge_hbm, clover_hbm, sign_hbm, null_hbm, ops_hbm,
    smooth_hbm, coarse_ref,
    src, gauge, clover, sign, null, ops,
    vb, rl, lf, cf, nf, of, s8, hb, acc_ref, ez,
    sx, st, rx, rt, wsum, sw, rw, gmat,
    in_sem, out_sem, send_sem, recv_sem,
):
    space = lax.axis_index("space")
    tm = lax.axis_index("tm")
    strides = STRIDES

    def ahead(d):
        if d == 3:
            return {"tm": lax.rem(tm + 1, n_tm)}
        return {"space": lax.rem(space + strides[d], n_space)}

    def behind(d):
        if d == 3:
            return {"tm": lax.rem(tm + n_tm - 1, n_tm)}
        return {"space": lax.rem(space + n_space - strides[d], n_space)}

    loads = [
        pltpu.make_async_copy(guess_hbm, vb.at[0], in_sem.at[0]),
        pltpu.make_async_copy(gauge_hbm, gauge, in_sem.at[1]),
        pltpu.make_async_copy(sign_hbm, sign, in_sem.at[2]),
        pltpu.make_async_copy(clover_hbm, clover, in_sem.at[3]),
        pltpu.make_async_copy(src_hbm, src, in_sem.at[4]),
        pltpu.make_async_copy(null_hbm, null, in_sem.at[5]),
        pltpu.make_async_copy(ops_hbm, ops, in_sem.at[6]),
    ]
    barrier = pltpu.get_barrier_semaphore()
    for d in range(4):
        for target in (ahead(d), behind(d)):
            pl.semaphore_signal(
                barrier, inc=1, device_id=target, device_id_type=pl.DeviceIdType.MESH
            )
    for load in loads:
        load.start()

    lane = lax.broadcasted_iota(jnp.int32, (8, 128), 1)
    row = lax.broadcasted_iota(jnp.int32, (8, 128), 0)
    lx = lane % 8
    ly = lane // 8 % 8
    low_half = lane < 64

    loads[1].wait()
    loads[2].wait()

    def widen_links(i, carry):
        rows = pl.ds(pl.multiple_of(i * 128, 128), 128)
        lf[rows, :] = gauge[rows, :].astype(F32)
        return carry

    lax.fori_loop(0, 9, widen_links, 0)
    sign_rows = (2 * sign[...] - 1).astype(F32)
    sign_rows = jnp.where(tm == n_tm - 1, sign_rows, jnp.ones_like(sign_rows))
    s8[pl.ds(0, 4, stride=2), :] = sign_rows
    s8[pl.ds(1, 4, stride=2), :] = sign_rows
    factor = s8[...]
    for rc in range(9):
        rows = pl.ds((27 + rc) * 32 + 24, 8)
        lf[rows, :] = lf[rows, :] * factor

    ez[...] = jnp.zeros_like(ez)
    hb[:, 0:PAD, :] = jnp.zeros((8, PAD, 128), F32)
    hb[:, PAD + 192 : PAD + 200, :] = jnp.zeros((8, 8, 128), F32)
    rt[:, :, 0:PAD, :] = jnp.zeros((3, 2, PAD, 128), F32)
    rt[:, :, PAD + 48 : PAD + 56, :] = jnp.zeros((3, 2, 8, 128), F32)

    def link(d, r, c, v):
        base = ((d * 9 + r * 3 + c) * 16 + 8 * v) * 2
        return lf[pl.ds(base, 8, stride=2), :], lf[pl.ds(base + 1, 8, stride=2), :]

    loads[0].wait()
    pl.semaphore_wait(barrier, 8)

    def exchange(i, d, forward):
        slot = 2 * d + (0 if forward else 1)
        if d == 3:
            source = st.at[i, slot - 6]
            target = rt.at[i, slot - 6, pl.ds(PAD, 48)]
        else:
            source = sx.at[i, slot]
            target = rx.at[i, slot]
        return pltpu.make_async_remote_copy(
            src_ref=source,
            dst_ref=target,
            send_sem=send_sem.at[i, slot],
            recv_sem=recv_sem.at[i, slot],
            device_id=behind(d) if forward else ahead(d),
            device_id_type=pl.DeviceIdType.MESH,
        )

    def prepare(i, d):
        width = 1 if d == 0 else 8
        which = lx if d == 0 else ly
        faces = {True: [], False: []}
        for v in range(2):
            spin = {}
            for p in range(2):
                for s in range(4):
                    for c in range(3):
                        spin[p, s, c] = vb[i, spinor_rows(p, s, c, v), :]
            half = {True: {}, False: {}}
            for a in range(2):
                source, phase = SPIN[d][a]
                for c in range(3):
                    up = spin[0, a, c], spin[1, a, c]
                    low = spin[0, source, c], spin[1, source, c]
                    half[True][a, c] = add_phase(up, low, NEG[phase])
                    half[False][a, c] = add_phase(up, low, phase)
            carried = {}
            for r in range(3):
                us = [link(d, c, r, v) for c in range(3)]
                for a in range(2):
                    total = None
                    for c in range(3):
                        total = mul_add(total, us[c], half[False][a, c], True)
                    carried[a, r] = total
            half[False] = carried
            for forward in (True, False):
                slot = 2 * d + (0 if forward else 1)
                for a in range(2):
                    for c in range(3):
                        for p in range(2):
                            j = (a * 3 + c) * 2 + p
                            value = half[forward][a, c][p]
                            hb[slot, pl.ds(PAD + j * 16 + 8 * v, 8), :] = value
                            faces[forward].append(value)
        for forward in (True, False):
            slot = 2 * d + (0 if forward else 1)
            values = faces[forward]
            if d < 2:
                for k in range(3):
                    packed = None
                    for m in range(8):
                        shift = m if forward else m - 7
                        moved = lane_roll(values[8 * k + m], width * shift)
                        packed = moved if packed is None else jnp.where(which == m, moved, packed)
                    sx[i, slot, pl.ds(8 * k, 8), :] = packed
            elif d == 2:
                take = 0 if forward else 3
                for j in range(6):
                    for v in range(2):
                        here, there = values[12 * v + j], lane_roll(values[12 * v + j + 6], 64)
                        pair = (
                            jnp.where(low_half, here, there)
                            if forward
                            else jnp.where(low_half, there, here)
                        )
                        ez[2, pl.ds(j * 16 + 8 * v, 8), :] = pair
                for k in range(3):
                    sx[i, slot, pl.ds(8 * k, 8), :] = ez[2, pl.ds(32 * k + take, 8, stride=4), :]
            else:
                for j in range(12):
                    st[i, slot - 6, pl.ds(4 * j, 4), :] = (
                        values[j][0:4, :] if forward else values[12 + j][4:8, :]
                    )
            exchange(i, d, forward).start()

    def shifted(i, d, forward, v):
        slot = 2 * d + (0 if forward else 1)
        out = []
        if d == 2 and v == 0:
            place = 3 if forward else 0
            for k in range(3):
                ez[1 - int(forward), pl.ds(32 * k + place, 8, stride=4), :] = rx[
                    i, slot, pl.ds(8 * k, 8), :
                ]
        for j in range(12):
            base = PAD + j * 16
            if d < 2:
                width = 1 if d == 0 else 8
                which = lx if d == 0 else ly
                m = v * 12 + j
                local = hb[slot, pl.ds(base + 8 * v, 8), :]
                packed = rx[i, slot, pl.ds(m // 8 * 8, 8), :]
                if forward:
                    remote = lane_roll(packed, width * (7 - m % 8))
                    out.append(jnp.where(which == 7, remote, lane_roll(local, -width)))
                else:
                    remote = lane_roll(packed, -width * (m % 8))
                    out.append(jnp.where(which == 0, remote, lane_roll(local, width)))
            elif d == 2:
                local = hb[slot, pl.ds(base + 8 * v, 8), :]
                remote = ez[1 - int(forward), pl.ds(j % 6 * 16 + 8 * v, 8), :]
                if j >= 6:
                    remote = lane_roll(remote, 64)
                if forward:
                    edge = jnp.where(row % 4 == 3, remote, row_roll(local, -1))
                    mixed = jnp.where(low_half, edge, local)
                else:
                    edge = jnp.where(row % 4 == 0, remote, row_roll(local, 1))
                    mixed = jnp.where(low_half, local, edge)
                out.append(lane_roll(mixed, 64))
            elif forward:
                if v == 0:
                    out.append(hb[slot, pl.ds(base + 4, 8), :])
                else:
                    local = hb[slot, pl.ds(base + 12, 8), :]
                    remote = rt[i, 0, pl.ds(PAD + 4 * j - 4, 8), :]
                    out.append(jnp.where(row < 4, local, remote))
            elif v == 1:
                out.append(hb[slot, pl.ds(base + 4, 8), :])
            else:
                local = hb[slot, pl.ds(base - 4, 8), :]
                remote = rt[i, 1, pl.ds(PAD + 4 * j, 8), :]
                out.append(jnp.where(row < 4, remote, local))
        return {(a, c): (out[(a * 3 + c) * 2], out[(a * 3 + c) * 2 + 1]) for a in range(2) for c in range(3)}

    def acc_rows(p, s, c, v):
        return pl.ds(((p * 4 + s) * 3 + c) * 16 + 8 * v, 8)

    def hop(i, d, store):
        exchange(i, d, True).wait_recv()
        exchange(i, d, False).wait_recv()
        for v in range(2):
            front = shifted(i, d, True, v)
            back = shifted(i, d, False, v)
            for r in range(3):
                us = [link(d, r, c, v) for c in range(3)]
                for a in range(2):
                    source, phase = SPIN[d][a]
                    w = None
                    for c in range(3):
                        w = mul_add(w, us[c], front[a, c], False)
                    b = back[a, r]
                    upper = acc_ref[acc_rows(0, a, r, v), :], acc_ref[acc_rows(1, a, r, v), :]
                    lower = (
                        acc_ref[acc_rows(0, source, r, v), :],
                        acc_ref[acc_rows(1, source, r, v), :],
                    )
                    upper = upper[0] + (w[0] + b[0]), upper[1] + (w[1] + b[1])
                    lower = add_phase(lower, (b[0] - w[0], b[1] - w[1]), CONJ[phase])
                    store(upper, a, r, v)
                    store(lower, source, r, v)

    def to_acc(value, s, c, v):
        acc_ref[acc_rows(0, s, c, v), :] = value[0]
        acc_ref[acc_rows(1, s, c, v), :] = value[1]

    def clover_term(i):
        for v in range(2):
            for b in range(2):
                x = [
                    tuple(vb[i, spinor_rows(p, 2 * b + n // 3, n % 3, v), :] for p in range(2))
                    for n in range(6)
                ]
                for r in range(6):
                    total = None
                    for n in range(6):
                        base = ((b * 36 + r * 6 + n) * 16 + 8 * v) * 2
                        c = cf[pl.ds(base, 8, stride=2), :], cf[pl.ds(base + 1, 8, stride=2), :]
                        total = mul_add(total, c, x[n], False)
                    s, c = 2 * b + r // 3, r % 3
                    f = tuple(src[spinor_rows(p, s, c, v), :] for p in range(2))
                    to_acc((2.0 * (f[0] - total[0]), 2.0 * (f[1] - total[1])), s, c, v)

    def widen_null(i, carry):
        rows = pl.ds(pl.multiple_of(i * 256, 256), 256)
        nf[rows, :] = null[rows, :].astype(F32)
        return carry

    def sweep(i, carry):
        prepare(i, 1)
        prepare(i, 0)
        prepare(i, 2)
        prepare(i, 3)

        @pl.when(i == 0)
        def _():
            loads[3].wait()
            loads[4].wait()

            def widen_clover(n, inner):
                rows = pl.ds(pl.multiple_of(n * 256, 256), 256)
                cf[rows, :] = clover[rows, :].astype(F32)
                return inner

            lax.fori_loop(0, 9, widen_clover, 0)

        clover_term(i)
        hop(i, 3, to_acc)
        hop(i, 0, to_acc)
        hop(i, 2, to_acc)

        @pl.when(i == 0)
        def _():
            loads[5].wait()

        lax.fori_loop(i * 12, i * 12 + 12, widen_null, 0)

        def finish(value, s, c, v):
            for p in range(2):
                rows = spinor_rows(p, s, c, v)
                vb[i + 1, rows, :] = vb[i, rows, :] + 0.08 * value[p]
                rl[rows, :] = (0.5 * value[p]).astype(BF16).astype(F32)

        hop(i, 1, finish)
        return carry

    lax.fori_loop(0, 3, sweep, 0)
    smooth = pltpu.make_async_copy(vb.at[2], smooth_hbm, out_sem.at[0])
    smooth.start()

    GROUP = 2

    def restrict(g, carry):
        sums = []
        for n in range(GROUP):
            kv = g * GROUP + n
            total = {}
            for az in range(2):
                re, im = None, None
                for c in range(3):
                    for t in range(4):
                        local = (2 * t + az) * 8
                        n_re = nf[pl.ds(pl.multiple_of((kv * 6 + c) * 64 + local, 8), 8), :]
                        n_im = nf[pl.ds(pl.multiple_of((kv * 6 + 3 + c) * 64 + local, 8), 8), :]
                        r_re = rl[pl.ds(c * 64 + local, 8), :]
                        r_im = rl[pl.ds((3 + c) * 64 + local, 8), :]
                        a = n_re * r_re + n_im * r_im
                        b = n_re * r_im - n_im * r_re
                        re = a if re is None else re + a
                        im = b if im is None else im + b
                total[0, az], total[1, az] = re, im
            sums += [total[0, 0], total[0, 1], total[1, 0], total[1, 1]]
        for bit in (1, 2, 4):
            first = row // bit % 2 == 0
            sums = [
                jnp.where(first, x, y) + row_roll(jnp.where(first, y, x), bit)
                for x, y in zip(sums[0::2], sums[1::2])
            ]
        wsum[pl.ds(pl.multiple_of(g * 8, 8), 8), :] = sums[0]
        return carry

    lax.fori_loop(0, NV // GROUP, restrict, 0)

    def split(x):
        high = x.astype(BF16)
        return high, (x - high.astype(F32)).astype(BF16)

    def dot_nt(a, b):
        return lax.dot_general(a, b, (((1,), (1,)), ((), ())), preferred_element_type=F32)

    lane16 = lax.broadcasted_iota(jnp.int32, (16, 128), 1)
    row16 = lax.broadcasted_iota(jnp.int32, (16, 128), 0)
    member = (lane16 // 32 % 2 * 2 + lane16 // 4 % 2 == row16).astype(F32).astype(BF16)
    out_lane = lax.broadcasted_iota(jnp.int32, (96, 512), 1)
    in_row = lax.broadcasted_iota(jnp.int32, (96, 512), 0)
    q = out_lane % 256 // 24
    match = (
        (in_row // 4 == out_lane % 256 % 24)
        & (in_row // 2 % 2 == out_lane // 256)
        & (in_row % 2 == q // 4)
        & (out_lane % 256 < 192)
    )
    gmat[...] = match.astype(F32).astype(BF16)
    high, low = split(wsum[...])
    partial = dot_nt(member, high) + dot_nt(member, low)
    high, low = split(partial)
    spread = jnp.dot(high, gmat[...], preferred_element_type=F32) + jnp.dot(
        low, gmat[...], preferred_element_type=F32
    )
    spread_lane = lax.broadcasted_iota(jnp.int32, (16, 512), 1)
    spread_row = lax.broadcasted_iota(jnp.int32, (16, 512), 0)
    vector = jnp.sum(
        jnp.where(spread_lane % 256 // 24 % 4 == spread_row, spread, 0.0), axis=0, keepdims=True
    )
    sw[0:1, :] = vector[:, 0:256]
    sw[1:2, :] = vector[:, 256:512]

    def exchange_coarse(d, forward):
        slot = 2 * d + (0 if forward else 1)
        return pltpu.make_async_remote_copy(
            src_ref=sw,
            dst_ref=rw.at[slot],
            send_sem=send_sem.at[3, slot],
            recv_sem=recv_sem.at[3, slot],
            device_id=behind(d) if forward else ahead(d),
            device_id_type=pl.DeviceIdType.MESH,
        )

    order = (1, 0, 2, 3)
    for d in order:
        for forward in (True, False):
            exchange_coarse(d, forward).start()

    loads[6].wait()
    for n in range(18):
        of[n] = ops[n].astype(F32)

    lane1 = lax.broadcasted_iota(jnp.int32, (8, 256), 1)
    own = jnp.broadcast_to(sw[0:1, :], (8, 256)), jnp.broadcast_to(sw[1:2, :], (8, 256))

    def apply(total, n, vec):
        w_re, w_im = vec[0][0:1, 0:192], vec[1][0:1, 0:192]
        o_re, o_im = of[2 * n], of[2 * n + 1]
        re = o_re * w_re - o_im * w_im
        im = o_re * w_im + o_im * w_re
        return (re, im) if total is None else (total[0] + re, total[1] + im)

    total = apply(None, 0, own)
    for d in (3, 0, 2, 1):
        for forward in (True, False):
            slot = 2 * d + (0 if forward else 1)
            exchange_coarse(d, forward).wait_recv()
            vec = []
            for p in range(2):
                remote = jnp.broadcast_to(rw[slot, p : p + 1, :], (8, 256))
                if d == 3:
                    vec.append(remote)
                    continue
                step = 1 << d
                near = lane1 // 24 // step % 2 == (0 if forward else 1)
                left = 256 - 24 * step
                right = 24 * step
                if forward:
                    vec.append(jnp.where(near, pltpu.roll(own[p], left, 1), pltpu.roll(remote, right, 1)))
                else:
                    vec.append(jnp.where(near, pltpu.roll(own[p], right, 1), pltpu.roll(remote, left, 1)))
            total = apply(total, 1 + slot, vec)

    segment = (
        lax.broadcasted_iota(jnp.int32, (16, 192), 1) // 24
        == lax.broadcasted_iota(jnp.int32, (16, 192), 0)
    )
    segment = segment.astype(F32).astype(BF16)
    for p in range(2):
        high, low = split(total[p])
        result = dot_nt(segment, high) + dot_nt(segment, low)
        coarse_ref[p] = result[0:8, :]

    smooth.wait()
    for d in range(4):
        for forward in (True, False):
            for i in range(3):
                exchange(i, d, forward).wait_send()
            exchange_coarse(d, forward).wait_send()


def solution(mesh):
    n_space, n_tm = mesh.shape["space"], mesh.shape["tm"]

    def spinor_in(x):
        return x.transpose(0, 2, 1, 3).reshape(6, 4, 16, 128).transpose(0, 2, 1, 3).reshape(384, 128)

    def spinor_out(x):
        return x.reshape(6, 16, 4, 128).transpose(0, 2, 1, 3).reshape(2, 3, 4, 2048).transpose(0, 2, 1, 3)

    def matrix_in(x, count):
        return (
            x.transpose(0, 2, 3, 1, 4)
            .reshape(count, 2, 16, 128)
            .transpose(0, 2, 1, 3)
            .reshape(count * 32, 128)
        )

    def on_device(source_field, initial_guess, gauge_links, clover, boundary_signs, null_vectors, coarse_ops):
        nulls = (
            null_vectors.transpose(0, 1, 3, 2, 4)
            .reshape(144, 4, 16, 128)
            .transpose(0, 2, 1, 3)
            .reshape(9216, 128)
        )
        vmem = pltpu.VMEM
        smoothed, coarse = pl.pallas_call(
            lambda *refs: kernel(n_space, n_tm, *refs),
            out_shape=(
                jax.ShapeDtypeStruct((384, 128), F32),
                jax.ShapeDtypeStruct((2, 8, 24), F32),
            ),
            in_specs=[pl.BlockSpec(memory_space=pl.ANY)] * 7,
            out_specs=(pl.BlockSpec(memory_space=pl.ANY), pl.BlockSpec(memory_space=vmem)),
            scratch_shapes=[
                vmem((384, 128), F32),
                vmem((1152, 128), BF16),
                vmem((2304, 128), BF16),
                vmem((4, 128), jnp.int32),
                vmem((9216, 128), BF16),
                vmem((18, 24, 192), BF16),
                vmem((4, 384, 128), F32),
                vmem((384, 128), F32),
                vmem((1152, 128), F32),
                vmem((2304, 128), F32),
                vmem((9216, 128), F32),
                vmem((18, 24, 192), F32),
                vmem((8, 128), F32),
                vmem((8, 208, 128), F32),
                vmem((384, 128), F32),
                vmem((3, 96, 128), F32),
                vmem((3, 6, 24, 128), F32),
                vmem((3, 2, 48, 128), F32),
                vmem((3, 6, 24, 128), F32),
                vmem((3, 2, 64, 128), F32),
                vmem((96, 128), F32),
                vmem((2, 256), F32),
                vmem((8, 2, 256), F32),
                vmem((96, 512), BF16),
                pltpu.SemaphoreType.DMA((7,)),
                pltpu.SemaphoreType.DMA((1,)),
                pltpu.SemaphoreType.DMA((4, 8)),
                pltpu.SemaphoreType.DMA((4, 8)),
            ],
            compiler_params=pltpu.CompilerParams(
                collective_id=0, has_side_effects=True, vmem_limit_bytes=60 * 1024 * 1024
            ),
        )(
            spinor_in(source_field),
            spinor_in(initial_guess),
            matrix_in(gauge_links, 36),
            matrix_in(clover, 72),
            boundary_signs.reshape(4, 128),
            nulls,
            coarse_ops.reshape(18, 24, 192),
        )
        return spinor_out(smoothed), coarse.transpose(0, 2, 1)

    field = P(None, None, None, ("tm", "space"))
    matrix = P(None, None, None, None, ("tm", "space"))
    return jax.shard_map(
        on_device,
        mesh=mesh,
        in_specs=(field, field, matrix, matrix, P("space"), matrix, field),
        out_specs=(field, P(None, None, ("tm", "space"))),
        check_vma=False,
    )
```

```python
import jax
import jax.numpy as jnp
from jax import lax
from jax.experimental import pallas as pl
from jax.experimental.pallas import tpu as pltpu
from jax.sharding import PartitionSpec as P

F32 = jnp.float32
BF16 = jnp.bfloat16
NV = 24
STRIDES = (32, 8, 1)
SPIN = (
    ((3, "-i"), (2, "-i")),
    ((3, "-1"), (2, "+1")),
    ((2, "-i"), (3, "+i")),
    ((2, "+1"), (3, "+1")),
)
CONJ = {"+1": "+1", "-1": "-1", "+i": "-i", "-i": "+i"}
NEG = {"+1": "-1", "-1": "+1", "+i": "-i", "-i": "+i"}
PAD = 8


def add_phase(acc, x, phase):
    if phase == "+1":
        return acc[0] + x[0], acc[1] + x[1]
    if phase == "-1":
        return acc[0] - x[0], acc[1] - x[1]
    if phase == "+i":
        return acc[0] - x[1], acc[1] + x[0]
    return acc[0] + x[1], acc[1] - x[0]


def lane_roll(x, shift):
    shift = shift % 128
    return x if shift == 0 else pltpu.roll(x, shift, 1)


def row_roll(x, shift):
    shift = shift % 8
    return x if shift == 0 else pltpu.roll(x, shift, 0)


def spinor_rows(p, s, c, v):
    return pl.ds(((p * 3 + c) * 16 + 8 * v) * 4 + s, 8, stride=4)


def mul_add(acc, a, b, conj):
    if conj:
        re, im = a[0] * b[0] + a[1] * b[1], a[0] * b[1] - a[1] * b[0]
    else:
        re, im = a[0] * b[0] - a[1] * b[1], a[0] * b[1] + a[1] * b[0]
    return (re, im) if acc is None else (acc[0] + re, acc[1] + im)


def kernel(
    n_space, n_tm,
    src_hbm, guess_hbm, gauge_hbm, clover_hbm, sign_hbm, null_hbm, ops_hbm,
    smooth_ref, coarse_ref,
    src, gauge, clover, sign, null, ops,
    vb, rl, lf, cf, nf, of, s8, hb, acc_ref, ez,
    sx, st, rx, rt, wsum, sw, rw, gmat,
    in_sem, send_sem, recv_sem,
):
    space = lax.axis_index("space")
    tm = lax.axis_index("tm")
    strides = STRIDES

    def ahead(d):
        if d == 3:
            return {"tm": lax.rem(tm + 1, n_tm)}
        return {"space": lax.rem(space + strides[d], n_space)}

    def behind(d):
        if d == 3:
            return {"tm": lax.rem(tm + n_tm - 1, n_tm)}
        return {"space": lax.rem(space + n_space - strides[d], n_space)}

    loads = [
        pltpu.make_async_copy(guess_hbm, vb.at[0], in_sem.at[0]),
        pltpu.make_async_copy(gauge_hbm, gauge, in_sem.at[1]),
        pltpu.make_async_copy(sign_hbm, sign, in_sem.at[2]),
        pltpu.make_async_copy(clover_hbm, clover, in_sem.at[3]),
        pltpu.make_async_copy(src_hbm, src, in_sem.at[4]),
        pltpu.make_async_copy(null_hbm, null, in_sem.at[5]),
        pltpu.make_async_copy(ops_hbm, ops, in_sem.at[6]),
    ]
    barrier = pltpu.get_barrier_semaphore()
    for d in range(4):
        for target in (ahead(d), behind(d)):
            pl.semaphore_signal(
                barrier, inc=1, device_id=target, device_id_type=pl.DeviceIdType.MESH
            )
    for load in loads:
        load.start()

    lane = lax.broadcasted_iota(jnp.int32, (8, 128), 1)
    row = lax.broadcasted_iota(jnp.int32, (8, 128), 0)
    lx = lane % 8
    ly = lane // 8 % 8
    low_half = lane < 64

    loads[1].wait()
    loads[2].wait()

    def widen_links(i, carry):
        rows = pl.ds(pl.multiple_of(i * 128, 128), 128)
        lf[rows, :] = gauge[rows, :].astype(F32)
        return carry

    lax.fori_loop(0, 9, widen_links, 0)
    sign_rows = (2 * sign[...] - 1).astype(F32)
    sign_rows = jnp.where(tm == n_tm - 1, sign_rows, jnp.ones_like(sign_rows))
    s8[pl.ds(0, 4, stride=2), :] = sign_rows
    s8[pl.ds(1, 4, stride=2), :] = sign_rows
    factor = s8[...]
    for rc in range(9):
        rows = pl.ds((27 + rc) * 32 + 24, 8)
        lf[rows, :] = lf[rows, :] * factor

    ez[...] = jnp.zeros_like(ez)
    hb[:, 0:PAD, :] = jnp.zeros((8, PAD, 128), F32)
    hb[:, PAD + 192 : PAD + 200, :] = jnp.zeros((8, 8, 128), F32)
    rt[:, :, 0:PAD, :] = jnp.zeros((3, 2, PAD, 128), F32)
    rt[:, :, PAD + 48 : PAD + 56, :] = jnp.zeros((3, 2, 8, 128), F32)

    def link(d, r, c, v):
        base = ((d * 9 + r * 3 + c) * 16 + 8 * v) * 2
        return lf[pl.ds(base, 8, stride=2), :], lf[pl.ds(base + 1, 8, stride=2), :]

    def exchange(i, d, forward):
        slot = 2 * d + (0 if forward else 1)
        if d == 3:
            source = st.at[i, slot - 6]
            target = rt.at[i, slot - 6, pl.ds(PAD, 48)]
        else:
            source = sx.at[i, slot]
            target = rx.at[i, slot]
        return pltpu.make_async_remote_copy(
            src_ref=source,
            dst_ref=target,
            send_sem=send_sem.at[i, slot],
            recv_sem=recv_sem.at[i, slot],
            device_id=behind(d) if forward else ahead(d),
            device_id_type=pl.DeviceIdType.MESH,
        )

    def prepare(i, d, read, keep, pack):
        width = 1 if d == 0 else 8
        which = lx if d == 0 else ly
        faces = {True: [], False: []}
        for v in range(2):
            spin = {}
            for p in range(2):
                for s in range(4):
                    for c in range(3):
                        spin[p, s, c] = read(p, s, c, v)
            half = {True: {}, False: {}}
            for a in range(2):
                source, phase = SPIN[d][a]
                for c in range(3):
                    up = spin[0, a, c], spin[1, a, c]
                    low = spin[0, source, c], spin[1, source, c]
                    half[True][a, c] = add_phase(up, low, NEG[phase])
                    half[False][a, c] = add_phase(up, low, phase)
            carried = {}
            for r in range(3):
                us = [link(d, c, r, v) for c in range(3)]
                for a in range(2):
                    total = None
                    for c in range(3):
                        total = mul_add(total, us[c], half[False][a, c], True)
                    carried[a, r] = total
            half[False] = carried
            for forward in (True, False):
                slot = 2 * d + (0 if forward else 1)
                for a in range(2):
                    for c in range(3):
                        for p in range(2):
                            j = (a * 3 + c) * 2 + p
                            value = half[forward][a, c][p]
                            if keep:
                                hb[slot, pl.ds(PAD + j * 16 + 8 * v, 8), :] = value
                            faces[forward].append(value)
        if not pack:
            return
        for forward in (True, False):
            slot = 2 * d + (0 if forward else 1)
            values = faces[forward]
            if d < 2:
                for k in range(3):
                    packed = None
                    for m in range(8):
                        shift = m if forward else m - 7
                        moved = lane_roll(values[8 * k + m], width * shift)
                        packed = moved if packed is None else jnp.where(which == m, moved, packed)
                    sx[i, slot, pl.ds(8 * k, 8), :] = packed
            elif d == 2:
                take = 0 if forward else 3
                for j in range(6):
                    for v in range(2):
                        here, there = values[12 * v + j], lane_roll(values[12 * v + j + 6], 64)
                        pair = (
                            jnp.where(low_half, here, there)
                            if forward
                            else jnp.where(low_half, there, here)
                        )
                        ez[2, pl.ds(j * 16 + 8 * v, 8), :] = pair
                for k in range(3):
                    sx[i, slot, pl.ds(8 * k, 8), :] = ez[2, pl.ds(32 * k + take, 8, stride=4), :]
            else:
                for j in range(12):
                    st[i, slot - 6, pl.ds(4 * j, 4), :] = (
                        values[j][0:4, :] if forward else values[12 + j][4:8, :]
                    )

    def send(i, d):
        for forward in (True, False):
            exchange(i, d, forward).start()

    def shifted(i, d, forward, v, part):
        slot = 2 * d + (0 if forward else 1)
        out = []
        if d == 2 and v == 0:
            place = 3 if forward else 0
            for k in range(3):
                ez[1 - int(forward), pl.ds(32 * k + place, 8, stride=4), :] = rx[
                    i, slot, pl.ds(8 * k, 8), :
                ]
        for j in range(12):
            base = PAD + j * 16
            if d < 2:
                width = 1 if d == 0 else 8
                which = lx if d == 0 else ly
                m = v * 12 + j
                local = hb[slot, pl.ds(base + 8 * v, 8), :]
                packed = rx[i, slot, pl.ds(m // 8 * 8, 8), :]
                edge = which == (7 if forward else 0)
                far = near = 0.0
                if part != "local":
                    far = lane_roll(packed, width * (7 - m % 8 if forward else -(m % 8)))
                if part != "remote":
                    near = lane_roll(local, -width if forward else width)
                out.append(jnp.where(edge, far, near))
            elif d == 2:
                local = hb[slot, pl.ds(base + 8 * v, 8), :]
                remote = ez[1 - int(forward), pl.ds(j % 6 * 16 + 8 * v, 8), :]
                if j >= 6:
                    remote = lane_roll(remote, 64)
                if forward:
                    edge = jnp.where(row % 4 == 3, remote, row_roll(local, -1))
                    mixed = jnp.where(low_half, edge, local)
                else:
                    edge = jnp.where(row % 4 == 0, remote, row_roll(local, 1))
                    mixed = jnp.where(low_half, local, edge)
                out.append(lane_roll(mixed, 64))
            elif forward:
                if v == 0:
                    out.append(hb[slot, pl.ds(base + 4, 8), :])
                else:
                    local = hb[slot, pl.ds(base + 12, 8), :]
                    remote = rt[i, 0, pl.ds(PAD + 4 * j - 4, 8), :]
                    out.append(jnp.where(row < 4, local, remote))
            elif v == 1:
                out.append(hb[slot, pl.ds(base + 4, 8), :])
            else:
                local = hb[slot, pl.ds(base - 4, 8), :]
                remote = rt[i, 1, pl.ds(PAD + 4 * j, 8), :]
                out.append(jnp.where(row < 4, remote, local))
        return {(a, c): (out[(a * 3 + c) * 2], out[(a * 3 + c) * 2 + 1]) for a in range(2) for c in range(3)}

    def acc_rows(p, s, c, v):
        return pl.ds(((p * 4 + s) * 3 + c) * 16 + 8 * v, 8)

    def hop(i, d, store, part="both"):
        if part != "local":
            exchange(i, d, True).wait_recv()
            exchange(i, d, False).wait_recv()
        for v in range(2):
            front = shifted(i, d, True, v, part)
            back = shifted(i, d, False, v, part)
            for r in range(3):
                us = [link(d, r, c, v) for c in range(3)]
                for a in range(2):
                    source, phase = SPIN[d][a]
                    w = None
                    for c in range(3):
                        w = mul_add(w, us[c], front[a, c], False)
                    b = back[a, r]
                    upper = acc_ref[acc_rows(0, a, r, v), :], acc_ref[acc_rows(1, a, r, v), :]
                    lower = (
                        acc_ref[acc_rows(0, source, r, v), :],
                        acc_ref[acc_rows(1, source, r, v), :],
                    )
                    upper = upper[0] + (w[0] + b[0]), upper[1] + (w[1] + b[1])
                    lower = add_phase(lower, (b[0] - w[0], b[1] - w[1]), CONJ[phase])
                    store(upper, a, r, v)
                    store(lower, source, r, v)

    def to_acc(value, s, c, v):
        acc_ref[acc_rows(0, s, c, v), :] = value[0]
        acc_ref[acc_rows(1, s, c, v), :] = value[1]

    def clover_term(i):
        for v in range(2):
            for b in range(2):
                x = [
                    tuple(vb[i, spinor_rows(p, 2 * b + n // 3, n % 3, v), :] for p in range(2))
                    for n in range(6)
                ]
                for r in range(6):
                    total = None
                    for n in range(6):
                        base = ((b * 36 + r * 6 + n) * 16 + 8 * v) * 2
                        c = cf[pl.ds(base, 8, stride=2), :], cf[pl.ds(base + 1, 8, stride=2), :]
                        total = mul_add(total, c, x[n], False)
                    s, c = 2 * b + r // 3, r % 3
                    f = tuple(src[spinor_rows(p, s, c, v), :] for p in range(2))
                    to_acc((2.0 * (f[0] - total[0]), 2.0 * (f[1] - total[1])), s, c, v)

    def widen_null(i, carry):
        rows = pl.ds(pl.multiple_of(i * 256, 256), 256)
        nf[rows, :] = null[rows, :].astype(F32)
        return carry

    def current(i):
        return lambda p, s, c, v: vb[i, spinor_rows(p, s, c, v), :]

    def without_y(i):
        return lambda p, s, c, v: vb[i, spinor_rows(p, s, c, v), :] + 0.08 * acc_ref[acc_rows(p, s, c, v), :]

    def sweep(i, last):
        clover_term(i)
        hop(i, 1, to_acc, "local")
        hop(i, 3, to_acc)
        hop(i, 0, to_acc)
        hop(i, 2, to_acc)
        if not last:
            prepare(i + 1, 1, without_y(i), False, True)
            send(i + 1, 1)

        def finish(value, s, c, v):
            for p in range(2):
                rows = spinor_rows(p, s, c, v)
                if last:
                    rl[rows, :] = (0.5 * value[p]).astype(BF16).astype(F32)
                else:
                    vb[i + 1, rows, :] = vb[i, rows, :] + 0.08 * value[p]

        hop(i, 1, finish, "remote")
        if not last:
            for d in (2, 0, 3):
                prepare(i + 1, d, current(i + 1), True, True)
                send(i + 1, d)
            prepare(i + 1, 1, current(i + 1), True, False)

    loads[0].wait()
    for d in (1, 2, 0, 3):
        prepare(0, d, current(0), True, True)
    pl.semaphore_wait(barrier, 8)
    for d in (1, 2, 0, 3):
        send(0, d)

    loads[3].wait()

    def widen_clover(n, carry):
        rows = pl.ds(pl.multiple_of(n * 256, 256), 256)
        cf[rows, :] = clover[rows, :].astype(F32)
        return carry

    lax.fori_loop(0, 9, widen_clover, 0)
    loads[5].wait()
    lax.fori_loop(0, 36, widen_null, 0)
    loads[6].wait()
    for n in range(18):
        of[n] = ops[n].astype(F32)
    out_lane = lax.broadcasted_iota(jnp.int32, (96, 512), 1)
    in_row = lax.broadcasted_iota(jnp.int32, (96, 512), 0)
    q = out_lane % 256 // 24
    match = (
        (in_row // 4 == out_lane % 256 % 24)
        & (in_row // 2 % 2 == out_lane // 256)
        & (in_row % 2 == q // 4)
        & (out_lane % 256 < 192)
    )
    gmat[...] = match.astype(F32).astype(BF16)
    loads[4].wait()

    def first_sweeps(i, carry):
        sweep(i, False)
        return carry

    lax.fori_loop(0, 2, first_sweeps, 0)
    smooth_ref[...] = vb[2]
    sweep(2, True)

    GROUP = 2

    def restrict(g, carry):
        sums = []
        for n in range(GROUP):
            kv = g * GROUP + n
            total = {}
            for az in range(2):
                re, im = None, None
                for c in range(3):
                    for t in range(4):
                        local = (2 * t + az) * 8
                        n_re = nf[pl.ds(pl.multiple_of((kv * 6 + c) * 64 + local, 8), 8), :]
                        n_im = nf[pl.ds(pl.multiple_of((kv * 6 + 3 + c) * 64 + local, 8), 8), :]
                        r_re = rl[pl.ds(c * 64 + local, 8), :]
                        r_im = rl[pl.ds((3 + c) * 64 + local, 8), :]
                        a = n_re * r_re + n_im * r_im
                        b = n_re * r_im - n_im * r_re
                        re = a if re is None else re + a
                        im = b if im is None else im + b
                total[0, az], total[1, az] = re, im
            sums += [total[0, 0], total[0, 1], total[1, 0], total[1, 1]]
        for bit in (1, 2, 4):
            first = row // bit % 2 == 0
            sums = [
                jnp.where(first, x, y) + row_roll(jnp.where(first, y, x), bit)
                for x, y in zip(sums[0::2], sums[1::2])
            ]
        wsum[pl.ds(pl.multiple_of(g * 8, 8), 8), :] = sums[0]
        return carry

    lax.fori_loop(0, NV // GROUP, restrict, 0)

    def split(x):
        high = x.astype(BF16)
        return high, (x - high.astype(F32)).astype(BF16)

    def dot_nt(a, b):
        return lax.dot_general(a, b, (((1,), (1,)), ((), ())), preferred_element_type=F32)

    lane16 = lax.broadcasted_iota(jnp.int32, (16, 128), 1)
    row16 = lax.broadcasted_iota(jnp.int32, (16, 128), 0)
    member = (lane16 // 32 % 2 * 2 + lane16 // 4 % 2 == row16).astype(F32).astype(BF16)
    high, low = split(wsum[...])
    partial = dot_nt(member, high) + dot_nt(member, low)
    high, low = split(partial)
    spread = jnp.dot(high, gmat[...], preferred_element_type=F32) + jnp.dot(
        low, gmat[...], preferred_element_type=F32
    )
    spread_lane = lax.broadcasted_iota(jnp.int32, (16, 512), 1)
    spread_row = lax.broadcasted_iota(jnp.int32, (16, 512), 0)
    vector = jnp.sum(
        jnp.where(spread_lane % 256 // 24 % 4 == spread_row, spread, 0.0), axis=0, keepdims=True
    )
    sw[0:1, :] = vector[:, 0:256]
    sw[1:2, :] = vector[:, 256:512]

    def exchange_coarse(d, forward):
        slot = 2 * d + (0 if forward else 1)
        return pltpu.make_async_remote_copy(
            src_ref=sw,
            dst_ref=rw.at[slot],
            send_sem=send_sem.at[3, slot],
            recv_sem=recv_sem.at[3, slot],
            device_id=behind(d) if forward else ahead(d),
            device_id_type=pl.DeviceIdType.MESH,
        )

    order = (1, 0, 2, 3)
    for d in order:
        for forward in (True, False):
            exchange_coarse(d, forward).start()

    lane1 = lax.broadcasted_iota(jnp.int32, (8, 256), 1)
    own = jnp.broadcast_to(sw[0:1, :], (8, 256)), jnp.broadcast_to(sw[1:2, :], (8, 256))

    def apply(total, n, vec):
        w_re, w_im = vec[0][0:1, 0:192], vec[1][0:1, 0:192]
        o_re, o_im = of[2 * n], of[2 * n + 1]
        re = o_re * w_re - o_im * w_im
        im = o_re * w_im + o_im * w_re
        return (re, im) if total is None else (total[0] + re, total[1] + im)

    total = apply(None, 0, own)
    for d in (3, 0, 2, 1):
        for forward in (True, False):
            slot = 2 * d + (0 if forward else 1)
            exchange_coarse(d, forward).wait_recv()
            vec = []
            for p in range(2):
                remote = jnp.broadcast_to(rw[slot, p : p + 1, :], (8, 256))
                if d == 3:
                    vec.append(remote)
                    continue
                step = 1 << d
                near = lane1 // 24 // step % 2 == (0 if forward else 1)
                left = 256 - 24 * step
                right = 24 * step
                if forward:
                    vec.append(jnp.where(near, pltpu.roll(own[p], left, 1), pltpu.roll(remote, right, 1)))
                else:
                    vec.append(jnp.where(near, pltpu.roll(own[p], right, 1), pltpu.roll(remote, left, 1)))
            total = apply(total, 1 + slot, vec)

    segment = (
        lax.broadcasted_iota(jnp.int32, (16, 192), 1) // 24
        == lax.broadcasted_iota(jnp.int32, (16, 192), 0)
    )
    segment = segment.astype(F32).astype(BF16)
    for p in range(2):
        high, low = split(total[p])
        result = dot_nt(segment, high) + dot_nt(segment, low)
        coarse_ref[p] = result[0:8, :]

    for d in range(4):
        for forward in (True, False):
            for i in range(3):
                exchange(i, d, forward).wait_send()
            exchange_coarse(d, forward).wait_send()


def hand_on(smooth_in, coarse_in, smooth_out, coarse_out, sem):
    copies = [
        pltpu.make_async_copy(smooth_in, smooth_out, sem.at[0]),
        pltpu.make_async_copy(coarse_in, coarse_out, sem.at[1]),
    ]
    for copy in copies:
        copy.start()
    for copy in copies:
        copy.wait()


def solution(mesh):
    n_space, n_tm = mesh.shape["space"], mesh.shape["tm"]

    def spinor_in(x):
        return x.transpose(0, 2, 1, 3).reshape(6, 4, 16, 128).transpose(0, 2, 1, 3).reshape(384, 128)

    def spinor_out(x):
        return x.reshape(6, 16, 4, 128).transpose(0, 2, 1, 3).reshape(2, 3, 4, 2048).transpose(0, 2, 1, 3)

    def matrix_in(x, count):
        return (
            x.transpose(0, 2, 3, 1, 4)
            .reshape(count, 2, 16, 128)
            .transpose(0, 2, 1, 3)
            .reshape(count * 32, 128)
        )

    def on_device(source_field, initial_guess, gauge_links, clover, boundary_signs, null_vectors, coarse_ops):
        nulls = (
            null_vectors.transpose(0, 1, 3, 2, 4)
            .reshape(144, 4, 16, 128)
            .transpose(0, 2, 1, 3)
            .reshape(9216, 128)
        )
        vmem = pltpu.VMEM
        smoothed, coarse = pl.pallas_call(
            lambda *refs: kernel(n_space, n_tm, *refs),
            out_shape=(
                jax.ShapeDtypeStruct((384, 128), F32),
                jax.ShapeDtypeStruct((2, 8, 24), F32),
            ),
            in_specs=[pl.BlockSpec(memory_space=pl.ANY)] * 7,
            out_specs=(pl.BlockSpec(memory_space=vmem), pl.BlockSpec(memory_space=vmem)),
            scratch_shapes=[
                vmem((384, 128), F32),
                vmem((1152, 128), BF16),
                vmem((2304, 128), BF16),
                vmem((4, 128), jnp.int32),
                vmem((9216, 128), BF16),
                vmem((18, 24, 192), BF16),
                vmem((4, 384, 128), F32),
                vmem((384, 128), F32),
                vmem((1152, 128), F32),
                vmem((2304, 128), F32),
                vmem((9216, 128), F32),
                vmem((18, 24, 192), F32),
                vmem((8, 128), F32),
                vmem((8, 208, 128), F32),
                vmem((384, 128), F32),
                vmem((3, 96, 128), F32),
                vmem((3, 6, 24, 128), F32),
                vmem((3, 2, 48, 128), F32),
                vmem((3, 6, 24, 128), F32),
                vmem((3, 2, 64, 128), F32),
                vmem((96, 128), F32),
                vmem((2, 256), F32),
                vmem((8, 2, 256), F32),
                vmem((96, 512), BF16),
                pltpu.SemaphoreType.DMA((7,)),
                pltpu.SemaphoreType.DMA((4, 8)),
                pltpu.SemaphoreType.DMA((4, 8)),
            ],
            compiler_params=pltpu.CompilerParams(
                collective_id=0, has_side_effects=True, vmem_limit_bytes=60 * 1024 * 1024
            ),
        )(
            spinor_in(source_field),
            spinor_in(initial_guess),
            matrix_in(gauge_links, 36),
            matrix_in(clover, 72),
            boundary_signs.reshape(4, 128),
            nulls,
            coarse_ops.reshape(18, 24, 192),
        )
        smoothed, coarse = pl.pallas_call(
            hand_on,
            out_shape=(
                jax.ShapeDtypeStruct((384, 128), F32),
                jax.ShapeDtypeStruct((2, 8, 24), F32),
            ),
            in_specs=[pl.BlockSpec(memory_space=vmem)] * 2,
            out_specs=[pl.BlockSpec(memory_space=pl.ANY)] * 2,
            scratch_shapes=[pltpu.SemaphoreType.DMA((2,))],
        )(smoothed, coarse)
        return spinor_out(smoothed), coarse.transpose(0, 2, 1)

    field = P(None, None, None, ("tm", "space"))
    matrix = P(None, None, None, None, ("tm", "space"))
    return jax.shard_map(
        on_device,
        mesh=mesh,
        in_specs=(field, field, matrix, matrix, P("space"), matrix, field),
        out_specs=(field, P(None, None, ("tm", "space"))),
        check_vma=False,
    )
```

```python
import jax
import jax.numpy as jnp
from jax import lax
from jax.experimental import pallas as pl
from jax.experimental.pallas import tpu as pltpu
from jax.sharding import PartitionSpec as P

F32 = jnp.float32
BF16 = jnp.bfloat16
NV = 24
STRIDES = (32, 8, 1)
SPIN = (
    ((3, "-i"), (2, "-i")),
    ((3, "-1"), (2, "+1")),
    ((2, "-i"), (3, "+i")),
    ((2, "+1"), (3, "+1")),
)
CONJ = {"+1": "+1", "-1": "-1", "+i": "-i", "-i": "+i"}
NEG = {"+1": "-1", "-1": "+1", "+i": "-i", "-i": "+i"}
PAD = 8


def add_phase(acc, x, phase):
    if phase == "+1":
        return acc[0] + x[0], acc[1] + x[1]
    if phase == "-1":
        return acc[0] - x[0], acc[1] - x[1]
    if phase == "+i":
        return acc[0] - x[1], acc[1] + x[0]
    return acc[0] + x[1], acc[1] - x[0]


def lane_roll(x, shift):
    shift = shift % 128
    return x if shift == 0 else pltpu.roll(x, shift, 1)


def row_roll(x, shift):
    shift = shift % 8
    return x if shift == 0 else pltpu.roll(x, shift, 0)


def spinor_rows(p, s, c, v):
    return pl.ds(((p * 3 + c) * 16 + 8 * v) * 4 + s, 8, stride=4)


def mul_add(acc, a, b, conj):
    if conj:
        re, im = a[0] * b[0] + a[1] * b[1], a[0] * b[1] - a[1] * b[0]
    else:
        re, im = a[0] * b[0] - a[1] * b[1], a[0] * b[1] + a[1] * b[0]
    return (re, im) if acc is None else (acc[0] + re, acc[1] + im)


def kernel(
    n_space, n_tm,
    src_hbm, guess_hbm, gauge_hbm, clover_hbm, sign_hbm, null_hbm, ops_hbm,
    smooth_ref, coarse_ref,
    src, gauge, clover, sign, null, ops,
    vb, rl, lf, cf, nf, of, s8, hb, acc_ref, ez,
    sx, st, rx, rt, wsum, inner, nb, rb, sw, rw, gmat,
    in_sem, send_sem, recv_sem,
):
    space = lax.axis_index("space")
    tm = lax.axis_index("tm")
    strides = STRIDES

    def ahead(d):
        if d == 3:
            return {"tm": lax.rem(tm + 1, n_tm)}
        return {"space": lax.rem(space + strides[d], n_space)}

    def behind(d):
        if d == 3:
            return {"tm": lax.rem(tm + n_tm - 1, n_tm)}
        return {"space": lax.rem(space + n_space - strides[d], n_space)}

    loads = [
        pltpu.make_async_copy(guess_hbm, vb.at[0], in_sem.at[0]),
        pltpu.make_async_copy(gauge_hbm, gauge, in_sem.at[1]),
        pltpu.make_async_copy(sign_hbm, sign, in_sem.at[2]),
        pltpu.make_async_copy(clover_hbm, clover, in_sem.at[3]),
        pltpu.make_async_copy(src_hbm, src, in_sem.at[4]),
        pltpu.make_async_copy(null_hbm, null, in_sem.at[5]),
        pltpu.make_async_copy(ops_hbm, ops, in_sem.at[6]),
    ]
    barrier = pltpu.get_barrier_semaphore()
    for d in (1, 2, 0, 3):
        for target in (ahead(d), behind(d)):
            pl.semaphore_signal(
                barrier, inc=1, device_id=target, device_id_type=pl.DeviceIdType.MESH
            )
    for load in loads:
        load.start()

    lane = lax.broadcasted_iota(jnp.int32, (8, 128), 1)
    row = lax.broadcasted_iota(jnp.int32, (8, 128), 0)
    lx = lane % 8
    ly = lane // 8 % 8
    low_half = lane < 64

    loads[1].wait()
    loads[2].wait()

    def widen_links(i, carry):
        rows = pl.ds(pl.multiple_of(i * 128, 128), 128)
        lf[rows, :] = gauge[rows, :].astype(F32)
        return carry

    lax.fori_loop(0, 9, widen_links, 0)
    sign_rows = (2 * sign[...] - 1).astype(F32)
    sign_rows = jnp.where(tm == n_tm - 1, sign_rows, jnp.ones_like(sign_rows))
    s8[pl.ds(0, 4, stride=2), :] = sign_rows
    s8[pl.ds(1, 4, stride=2), :] = sign_rows
    factor = s8[...]
    for rc in range(9):
        rows = pl.ds((27 + rc) * 32 + 24, 8)
        lf[rows, :] = lf[rows, :] * factor

    ez[...] = jnp.zeros_like(ez)
    hb[:, 0:PAD, :] = jnp.zeros((8, PAD, 128), F32)
    hb[:, PAD + 192 : PAD + 200, :] = jnp.zeros((8, 8, 128), F32)
    rt[:, :, 0:PAD, :] = jnp.zeros((3, 2, PAD, 128), F32)
    rt[:, :, PAD + 48 : PAD + 56, :] = jnp.zeros((3, 2, 8, 128), F32)

    def link(d, r, c, v):
        base = ((d * 9 + r * 3 + c) * 16 + 8 * v) * 2
        return lf[pl.ds(base, 8, stride=2), :], lf[pl.ds(base + 1, 8, stride=2), :]

    def exchange(i, d, forward):
        slot = 2 * d + (0 if forward else 1)
        if d == 3:
            source = st.at[i, slot - 6]
            target = rt.at[i, slot - 6, pl.ds(PAD, 48)]
        else:
            source = sx.at[i, slot]
            target = rx.at[i, slot]
        return pltpu.make_async_remote_copy(
            src_ref=source,
            dst_ref=target,
            send_sem=send_sem.at[i, slot],
            recv_sem=recv_sem.at[i, slot],
            device_id=behind(d) if forward else ahead(d),
            device_id_type=pl.DeviceIdType.MESH,
        )

    def prepare(i, d, read, keep, pack):
        width = 1 if d == 0 else 8
        which = lx if d == 0 else ly
        faces = {True: [], False: []}
        for v in range(2):
            spin = {}
            for p in range(2):
                for s in range(4):
                    for c in range(3):
                        spin[p, s, c] = read(p, s, c, v)
            half = {True: {}, False: {}}
            for a in range(2):
                source, phase = SPIN[d][a]
                for c in range(3):
                    up = spin[0, a, c], spin[1, a, c]
                    low = spin[0, source, c], spin[1, source, c]
                    half[True][a, c] = add_phase(up, low, NEG[phase])
                    half[False][a, c] = add_phase(up, low, phase)
            carried = {}
            for r in range(3):
                us = [link(d, c, r, v) for c in range(3)]
                for a in range(2):
                    total = None
                    for c in range(3):
                        total = mul_add(total, us[c], half[False][a, c], True)
                    carried[a, r] = total
            half[False] = carried
            for forward in (True, False):
                slot = 2 * d + (0 if forward else 1)
                for a in range(2):
                    for c in range(3):
                        for p in range(2):
                            j = (a * 3 + c) * 2 + p
                            value = half[forward][a, c][p]
                            if keep:
                                hb[slot, pl.ds(PAD + j * 16 + 8 * v, 8), :] = value
                            faces[forward].append(value)
        if not pack:
            return
        for forward in (True, False):
            slot = 2 * d + (0 if forward else 1)
            values = faces[forward]
            if d < 2:
                for k in range(3):
                    packed = None
                    for m in range(8):
                        shift = m if forward else m - 7
                        moved = lane_roll(values[8 * k + m], width * shift)
                        packed = moved if packed is None else jnp.where(which == m, moved, packed)
                    sx[i, slot, pl.ds(8 * k, 8), :] = packed
            elif d == 2:
                take = 0 if forward else 3
                for j in range(6):
                    for v in range(2):
                        here, there = values[12 * v + j], lane_roll(values[12 * v + j + 6], 64)
                        pair = (
                            jnp.where(low_half, here, there)
                            if forward
                            else jnp.where(low_half, there, here)
                        )
                        ez[2, pl.ds(j * 16 + 8 * v, 8), :] = pair
                for k in range(3):
                    sx[i, slot, pl.ds(8 * k, 8), :] = ez[2, pl.ds(32 * k + take, 8, stride=4), :]
            else:
                for j in range(12):
                    st[i, slot - 6, pl.ds(4 * j, 4), :] = (
                        values[j][0:4, :] if forward else values[12 + j][4:8, :]
                    )

    def send(i, d):
        for forward in (True, False):
            exchange(i, d, forward).start()

    def shifted(i, d, forward, v, part):
        slot = 2 * d + (0 if forward else 1)
        out = []
        if d == 2 and v == 0:
            place = 3 if forward else 0
            for k in range(3):
                ez[1 - int(forward), pl.ds(32 * k + place, 8, stride=4), :] = rx[
                    i, slot, pl.ds(8 * k, 8), :
                ]
        for j in range(12):
            base = PAD + j * 16
            if d < 2:
                width = 1 if d == 0 else 8
                which = lx if d == 0 else ly
                m = v * 12 + j
                local = hb[slot, pl.ds(base + 8 * v, 8), :]
                packed = rx[i, slot, pl.ds(m // 8 * 8, 8), :]
                edge = which == (7 if forward else 0)
                far = near = 0.0
                if part != "local":
                    far = lane_roll(packed, width * (7 - m % 8 if forward else -(m % 8)))
                if part != "remote":
                    near = lane_roll(local, -width if forward else width)
                out.append(jnp.where(edge, far, near))
            elif d == 2:
                local = hb[slot, pl.ds(base + 8 * v, 8), :]
                remote = ez[1 - int(forward), pl.ds(j % 6 * 16 + 8 * v, 8), :]
                if j >= 6:
                    remote = lane_roll(remote, 64)
                if forward:
                    edge = jnp.where(row % 4 == 3, remote, row_roll(local, -1))
                    mixed = jnp.where(low_half, edge, local)
                else:
                    edge = jnp.where(row % 4 == 0, remote, row_roll(local, 1))
                    mixed = jnp.where(low_half, local, edge)
                out.append(lane_roll(mixed, 64))
            elif forward:
                if v == 0:
                    out.append(hb[slot, pl.ds(base + 4, 8), :])
                else:
                    local = hb[slot, pl.ds(base + 12, 8), :]
                    remote = rt[i, 0, pl.ds(PAD + 4 * j - 4, 8), :]
                    out.append(jnp.where(row < 4, local, remote))
            elif v == 1:
                out.append(hb[slot, pl.ds(base + 4, 8), :])
            else:
                local = hb[slot, pl.ds(base - 4, 8), :]
                remote = rt[i, 1, pl.ds(PAD + 4 * j, 8), :]
                out.append(jnp.where(row < 4, remote, local))
        return {(a, c): (out[(a * 3 + c) * 2], out[(a * 3 + c) * 2 + 1]) for a in range(2) for c in range(3)}

    def acc_rows(p, s, c, v):
        return pl.ds(((p * 4 + s) * 3 + c) * 16 + 8 * v, 8)

    def hop(i, d, store, part="both"):
        if part != "local":
            exchange(i, d, True).wait_recv()
            exchange(i, d, False).wait_recv()
        for v in range(2):
            front = shifted(i, d, True, v, part)
            back = shifted(i, d, False, v, part)
            for r in range(3):
                us = [link(d, r, c, v) for c in range(3)]
                for a in range(2):
                    source, phase = SPIN[d][a]
                    w = None
                    for c in range(3):
                        w = mul_add(w, us[c], front[a, c], False)
                    b = back[a, r]
                    upper = acc_ref[acc_rows(0, a, r, v), :], acc_ref[acc_rows(1, a, r, v), :]
                    lower = (
                        acc_ref[acc_rows(0, source, r, v), :],
                        acc_ref[acc_rows(1, source, r, v), :],
                    )
                    upper = upper[0] + (w[0] + b[0]), upper[1] + (w[1] + b[1])
                    lower = add_phase(lower, (b[0] - w[0], b[1] - w[1]), CONJ[phase])
                    store(upper, a, r, v)
                    store(lower, source, r, v)

    def to_acc(value, s, c, v):
        acc_ref[acc_rows(0, s, c, v), :] = value[0]
        acc_ref[acc_rows(1, s, c, v), :] = value[1]

    def clover_term(i):
        for v in range(2):
            for b in range(2):
                x = [
                    tuple(vb[i, spinor_rows(p, 2 * b + n // 3, n % 3, v), :] for p in range(2))
                    for n in range(6)
                ]
                for r in range(6):
                    total = None
                    for n in range(6):
                        base = ((b * 36 + r * 6 + n) * 16 + 8 * v) * 2
                        c = cf[pl.ds(base, 8, stride=2), :], cf[pl.ds(base + 1, 8, stride=2), :]
                        total = mul_add(total, c, x[n], False)
                    s, c = 2 * b + r // 3, r % 3
                    f = tuple(src[spinor_rows(p, s, c, v), :] for p in range(2))
                    to_acc((2.0 * (f[0] - total[0]), 2.0 * (f[1] - total[1])), s, c, v)

    def widen_null(i, carry):
        rows = pl.ds(pl.multiple_of(i * 256, 256), 256)
        nf[rows, :] = null[rows, :].astype(F32)
        return carry

    def current(i):
        return lambda p, s, c, v: vb[i, spinor_rows(p, s, c, v), :]

    def without_y(i):
        return lambda p, s, c, v: vb[i, spinor_rows(p, s, c, v), :] + 0.08 * acc_ref[acc_rows(p, s, c, v), :]

    GROUP = 2

    def restrict(null_ref, res_ref, steps, part, unroll):
        def group(g, carry):
            sums = []
            for n in range(GROUP):
                kv = g * GROUP + n
                total = {}
                for az in range(2):
                    re, im = None, None
                    for c in range(3):
                        for t in range(steps):
                            at = c * 16 * steps + (2 * t + az) * 8
                            half = 48 * steps
                            base = kv * 96 * steps + at
                            n_re = null_ref[pl.ds(pl.multiple_of(base, 8), 8), :]
                            n_im = null_ref[pl.ds(pl.multiple_of(base + half, 8), 8), :]
                            r_re = res_ref[pl.ds(at, 8), :]
                            r_im = res_ref[pl.ds(half + at, 8), :]
                            x = n_re * r_re + n_im * r_im
                            y = n_re * r_im - n_im * r_re
                            re = x if re is None else re + x
                            im = y if im is None else im + y
                    total[0, az], total[1, az] = re, im
                sums += [total[0, 0], total[0, 1], total[1, 0], total[1, 1]]
            for bit in (1, 2, 4):
                first = row // bit % 2 == 0
                sums = [
                    jnp.where(first, x, y) + row_roll(jnp.where(first, y, x), bit)
                    for x, y in zip(sums[0::2], sums[1::2])
                ]
            wsum[part, pl.ds(pl.multiple_of(g * 8, 8), 8), :] = sums[0]
            return carry

        lax.fori_loop(0, NV // GROUP, group, 0, unroll=unroll)

    side = [((lane // 8 - 2 * t) % 8 == 0) | ((lane // 8 - 2 * t) % 8 == 7) for t in range(4)]

    def fold(parts):
        out = parts[0]
        for t in range(1, 4):
            out = jnp.where(side[t], lane_roll(parts[t], 16 * t), out)
        return out

    def fold_null(n, carry):
        for az in range(2):
            parts = [nf[pl.ds(pl.multiple_of(n * 64 + (2 * t + az) * 8, 8), 8), :] for t in range(4)]
            nb[pl.ds(pl.multiple_of(n * 16 + az * 8, 8), 8), :] = fold(parts)
        return carry

    def split(x):
        high = x.astype(BF16)
        return jnp.concatenate([high, (x - high.astype(F32)).astype(BF16)], axis=1)

    def dot_nt(a, b):
        return lax.dot_general(a, b, (((1,), (1,)), ((), ())), preferred_element_type=F32)

    def sums_of(part, member):
        return dot_nt(member, split(wsum[part]))

    lane16 = lax.broadcasted_iota(jnp.int32, (16, 256), 1) % 128
    row16 = lax.broadcasted_iota(jnp.int32, (16, 256), 0)
    inner_member = (lane16 // 32 % 2 * 2 + lane16 // 4 % 2 == row16).astype(F32).astype(BF16)
    outer_member = (lane16 // 8 % 2 * 2 + lane16 // 4 % 2 == row16).astype(F32).astype(BF16)
    spread_lane = lax.broadcasted_iota(jnp.int32, (16, 512), 1)
    spread_row = lax.broadcasted_iota(jnp.int32, (16, 512), 0)
    spread_mask = spread_lane % 256 // 24 % 4 == spread_row

    def inner_layers():
        for p in range(2):
            for s in range(4):
                for c in range(3):
                    for v in range(2):
                        value = 0.5 * acc_ref[acc_rows(p, s, c, v), :]
                        value = jnp.where((ly == 0) | (ly == 7), 0.0, value)
                        rl[spinor_rows(p, s, c, v), :] = value.astype(BF16).astype(F32)
        restrict(nf, rl, 4, 0, 1)
        inner[...] = sums_of(0, inner_member)

    def sweep(i, last):
        clover_term(i)
        hop(i, 1, to_acc, "local")
        hop(i, 3, to_acc)
        hop(i, 0, to_acc)
        hop(i, 2, to_acc)
        if not last:
            prepare(i + 1, 1, without_y(i), False, True)
            send(i + 1, 1)
        else:
            inner_layers()

        def finish(value, s, c, v):
            for p in range(2):
                rows = spinor_rows(p, s, c, v)
                if last:
                    rl[rows, :] = (0.5 * value[p]).astype(BF16).astype(F32)
                else:
                    vb[i + 1, rows, :] = vb[i, rows, :] + 0.08 * value[p]

        hop(i, 1, finish, "remote")
        if not last:
            for d in (2, 0, 3):
                prepare(i + 1, d, current(i + 1), True, True)
                send(i + 1, d)
            prepare(i + 1, 1, current(i + 1), True, False)

    loads[0].wait()
    for d in (1, 2, 0, 3):
        prepare(0, d, current(0), True, True)
    pl.semaphore_wait(barrier, 8)
    for d in (1, 2, 0, 3):
        send(0, d)

    loads[3].wait()

    def widen_clover(n, carry):
        rows = pl.ds(pl.multiple_of(n * 256, 256), 256)
        cf[rows, :] = clover[rows, :].astype(F32)
        return carry

    lax.fori_loop(0, 9, widen_clover, 0)
    loads[5].wait()
    lax.fori_loop(0, 36, widen_null, 0)
    loads[6].wait()
    for n in range(18):
        of[n] = ops[n].astype(F32)
    out_lane = lax.broadcasted_iota(jnp.int32, (256, 512), 1)
    in_row = lax.broadcasted_iota(jnp.int32, (256, 512), 0) % 128
    q = out_lane % 256 // 24
    match = (
        (in_row // 4 == out_lane % 256 % 24)
        & (in_row // 2 % 2 == out_lane // 256)
        & (in_row % 2 == q // 4)
        & (out_lane % 256 < 192)
        & (in_row < 96)
    )
    gmat[...] = match.astype(F32).astype(BF16)
    wsum[:, 96:128, :] = jnp.zeros((2, 32, 128), F32)
    lax.fori_loop(0, 144, fold_null, 0, unroll=16)
    loads[4].wait()

    def first_sweeps(i, carry):
        sweep(i, False)
        return carry

    lax.fori_loop(0, 2, first_sweeps, 0)
    smooth_ref[...] = vb[2]
    sweep(2, True)

    for n in range(6):
        for az in range(2):
            rb[pl.ds((n * 2 + az) * 8, 8), :] = fold(
                [rl[pl.ds(n * 64 + (2 * t + az) * 8, 8), :] for t in range(4)]
            )
    restrict(nb, rb, 1, 1, 12)
    partial = sums_of(1, outer_member) + inner[...]

    spread = jnp.dot(split(partial), gmat[...], preferred_element_type=F32)
    vector = jnp.sum(jnp.where(spread_mask, spread, 0.0), axis=0, keepdims=True)
    sw[0:1, :] = vector[:, 0:256]
    sw[1:2, :] = vector[:, 256:512]

    def exchange_coarse(d, forward):
        slot = 2 * d + (0 if forward else 1)
        return pltpu.make_async_remote_copy(
            src_ref=sw,
            dst_ref=rw.at[slot],
            send_sem=send_sem.at[3, slot],
            recv_sem=recv_sem.at[3, slot],
            device_id=behind(d) if forward else ahead(d),
            device_id_type=pl.DeviceIdType.MESH,
        )

    order = (1, 0, 2, 3)
    for d in order:
        for forward in (True, False):
            exchange_coarse(d, forward).start()

    lane1 = lax.broadcasted_iota(jnp.int32, (8, 256), 1)
    own = jnp.broadcast_to(sw[0:1, :], (8, 256)), jnp.broadcast_to(sw[1:2, :], (8, 256))

    def apply(total, n, vec):
        w_re, w_im = vec[0][0:1, 0:192], vec[1][0:1, 0:192]
        o_re, o_im = of[2 * n], of[2 * n + 1]
        re = o_re * w_re - o_im * w_im
        im = o_re * w_im + o_im * w_re
        return (re, im) if total is None else (total[0] + re, total[1] + im)

    total = apply(None, 0, own)
    for d in (3, 0, 2, 1):
        for forward in (True, False):
            slot = 2 * d + (0 if forward else 1)
            exchange_coarse(d, forward).wait_recv()
            vec = []
            for p in range(2):
                remote = jnp.broadcast_to(rw[slot, p : p + 1, :], (8, 256))
                if d == 3:
                    vec.append(remote)
                    continue
                step = 1 << d
                near = lane1 // 24 // step % 2 == (0 if forward else 1)
                left = 256 - 24 * step
                right = 24 * step
                if forward:
                    vec.append(jnp.where(near, pltpu.roll(own[p], left, 1), pltpu.roll(remote, right, 1)))
                else:
                    vec.append(jnp.where(near, pltpu.roll(own[p], right, 1), pltpu.roll(remote, left, 1)))
            total = apply(total, 1 + slot, vec)

    seg_lane = lax.broadcasted_iota(jnp.int32, (16, 192), 1)
    segment = (seg_lane // 24 == lax.broadcasted_iota(jnp.int32, (16, 192), 0)).astype(F32).astype(BF16)
    for p in range(2):
        high = total[p].astype(BF16)
        low = (total[p] - high.astype(F32)).astype(BF16)
        result = dot_nt(segment, high) + dot_nt(segment, low)
        coarse_ref[p] = result[0:8, :]

    for d in range(4):
        for forward in (True, False):
            for i in range(3):
                exchange(i, d, forward).wait_send()
            exchange_coarse(d, forward).wait_send()


def hand_on(smooth_in, coarse_in, smooth_out, coarse_out, sem):
    copies = [
        pltpu.make_async_copy(smooth_in, smooth_out, sem.at[0]),
        pltpu.make_async_copy(coarse_in, coarse_out, sem.at[1]),
    ]
    for copy in copies:
        copy.start()
    for copy in copies:
        copy.wait()


def solution(mesh):
    n_space, n_tm = mesh.shape["space"], mesh.shape["tm"]

    def spinor_in(x):
        return x.transpose(0, 2, 1, 3).reshape(6, 4, 16, 128).transpose(0, 2, 1, 3).reshape(384, 128)

    def spinor_out(x):
        return x.reshape(6, 16, 4, 128).transpose(0, 2, 1, 3).reshape(2, 3, 4, 2048).transpose(0, 2, 1, 3)

    def matrix_in(x, count):
        return (
            x.transpose(0, 2, 3, 1, 4)
            .reshape(count, 2, 16, 128)
            .transpose(0, 2, 1, 3)
            .reshape(count * 32, 128)
        )

    def on_device(source_field, initial_guess, gauge_links, clover, boundary_signs, null_vectors, coarse_ops):
        nulls = (
            null_vectors.transpose(0, 1, 3, 2, 4)
            .reshape(144, 4, 16, 128)
            .transpose(0, 2, 1, 3)
            .reshape(9216, 128)
        )
        vmem = pltpu.VMEM
        smoothed, coarse = pl.pallas_call(
            lambda *refs: kernel(n_space, n_tm, *refs),
            out_shape=(
                jax.ShapeDtypeStruct((384, 128), F32),
                jax.ShapeDtypeStruct((2, 8, 24), F32),
            ),
            in_specs=[pl.BlockSpec(memory_space=pl.ANY)] * 7,
            out_specs=(pl.BlockSpec(memory_space=vmem), pl.BlockSpec(memory_space=vmem)),
            scratch_shapes=[
                vmem((384, 128), F32),
                vmem((1152, 128), BF16),
                vmem((2304, 128), BF16),
                vmem((4, 128), jnp.int32),
                vmem((9216, 128), BF16),
                vmem((18, 24, 192), BF16),
                vmem((4, 384, 128), F32),
                vmem((384, 128), F32),
                vmem((1152, 128), F32),
                vmem((2304, 128), F32),
                vmem((9216, 128), F32),
                vmem((18, 24, 192), F32),
                vmem((8, 128), F32),
                vmem((8, 208, 128), F32),
                vmem((384, 128), F32),
                vmem((3, 96, 128), F32),
                vmem((3, 6, 24, 128), F32),
                vmem((3, 2, 48, 128), F32),
                vmem((3, 6, 24, 128), F32),
                vmem((3, 2, 64, 128), F32),
                vmem((2, 128, 128), F32),
                vmem((16, 128), F32),
                vmem((2304, 128), F32),
                vmem((96, 128), F32),
                vmem((2, 256), F32),
                vmem((8, 2, 256), F32),
                vmem((256, 512), BF16),
                pltpu.SemaphoreType.DMA((7,)),
                pltpu.SemaphoreType.DMA((4, 8)),
                pltpu.SemaphoreType.DMA((4, 8)),
            ],
            compiler_params=pltpu.CompilerParams(
                collective_id=0, has_side_effects=True, vmem_limit_bytes=60 * 1024 * 1024
            ),
        )(
            spinor_in(source_field),
            spinor_in(initial_guess),
            matrix_in(gauge_links, 36),
            matrix_in(clover, 72),
            boundary_signs.reshape(4, 128),
            nulls,
            coarse_ops.reshape(18, 24, 192),
        )
        smoothed, coarse = pl.pallas_call(
            hand_on,
            out_shape=(
                jax.ShapeDtypeStruct((384, 128), F32),
                jax.ShapeDtypeStruct((2, 8, 24), F32),
            ),
            in_specs=[pl.BlockSpec(memory_space=vmem)] * 2,
            out_specs=[pl.BlockSpec(memory_space=pl.ANY)] * 2,
            scratch_shapes=[pltpu.SemaphoreType.DMA((2,))],
        )(smoothed, coarse)
        return spinor_out(smoothed), coarse.transpose(0, 2, 1)

    field = P(None, None, None, ("tm", "space"))
    matrix = P(None, None, None, None, ("tm", "space"))
    return jax.shard_map(
        on_device,
        mesh=mesh,
        in_specs=(field, field, matrix, matrix, P("space"), matrix, field),
        out_specs=(field, P(None, None, ("tm", "space"))),
        check_vma=False,
    )
```

```python
import jax
import jax.numpy as jnp
from jax import lax
from jax.experimental import pallas as pl
from jax.experimental.pallas import tpu as pltpu
from jax.sharding import PartitionSpec as P

F32 = jnp.float32
BF16 = jnp.bfloat16
NV = 24
STRIDES = (32, 8, 1)
SPIN = (
    ((3, "-i"), (2, "-i")),
    ((3, "-1"), (2, "+1")),
    ((2, "-i"), (3, "+i")),
    ((2, "+1"), (3, "+1")),
)
CONJ = {"+1": "+1", "-1": "-1", "+i": "-i", "-i": "+i"}
NEG = {"+1": "-1", "-1": "+1", "+i": "-i", "-i": "+i"}
PAD = 8


def add_phase(acc, x, phase):
    if phase == "+1":
        return acc[0] + x[0], acc[1] + x[1]
    if phase == "-1":
        return acc[0] - x[0], acc[1] - x[1]
    if phase == "+i":
        return acc[0] - x[1], acc[1] + x[0]
    return acc[0] + x[1], acc[1] - x[0]


def lane_roll(x, shift):
    shift = shift % 128
    return x if shift == 0 else pltpu.roll(x, shift, 1)


def row_roll(x, shift):
    shift = shift % 8
    return x if shift == 0 else pltpu.roll(x, shift, 0)


def spinor_rows(p, s, c, v):
    return pl.ds(((p * 3 + c) * 16 + 8 * v) * 4 + s, 8, stride=4)


def mul_add(acc, a, b, conj):
    if conj:
        re, im = a[0] * b[0] + a[1] * b[1], a[0] * b[1] - a[1] * b[0]
    else:
        re, im = a[0] * b[0] - a[1] * b[1], a[0] * b[1] + a[1] * b[0]
    return (re, im) if acc is None else (acc[0] + re, acc[1] + im)


def kernel(
    n_space, n_tm,
    src_hbm, guess_hbm, gauge_hbm, clover_hbm, sign_hbm, null_hbm, ops_hbm,
    smooth_ref, coarse_ref,
    src, gauge, clover, sign, null, ops,
    vb, rl, lf, cf, nf, of, s8, hb, acc_ref, ez,
    sx, st, rx, rt, wsum, inner, nb, rb, sw, rw, gmat,
    in_sem, send_sem, recv_sem,
):
    space = lax.axis_index("space")
    tm = lax.axis_index("tm")
    strides = STRIDES

    def ahead(d):
        if d == 3:
            return {"tm": lax.rem(tm + 1, n_tm)}
        return {"space": lax.rem(space + strides[d], n_space)}

    def behind(d):
        if d == 3:
            return {"tm": lax.rem(tm + n_tm - 1, n_tm)}
        return {"space": lax.rem(space + n_space - strides[d], n_space)}

    loads = [
        pltpu.make_async_copy(guess_hbm, vb.at[0], in_sem.at[0]),
        pltpu.make_async_copy(gauge_hbm, gauge, in_sem.at[1]),
        pltpu.make_async_copy(sign_hbm, sign, in_sem.at[2]),
        pltpu.make_async_copy(clover_hbm, clover, in_sem.at[3]),
        pltpu.make_async_copy(src_hbm, src, in_sem.at[4]),
        pltpu.make_async_copy(null_hbm, null, in_sem.at[5]),
        pltpu.make_async_copy(ops_hbm, ops, in_sem.at[6]),
    ]
    barrier = pltpu.get_barrier_semaphore()
    for d in (1, 2, 0, 3):
        for target in (ahead(d), behind(d)):
            pl.semaphore_signal(
                barrier, inc=1, device_id=target, device_id_type=pl.DeviceIdType.MESH
            )
    for load in loads:
        load.start()

    lane = lax.broadcasted_iota(jnp.int32, (8, 128), 1)
    row = lax.broadcasted_iota(jnp.int32, (8, 128), 0)
    lx = lane % 8
    ly = lane // 8 % 8
    low_half = lane < 64

    loads[1].wait()
    loads[2].wait()

    def widen_links(i, carry):
        rows = pl.ds(pl.multiple_of(i * 128, 128), 128)
        lf[rows, :] = gauge[rows, :].astype(F32)
        return carry

    lax.fori_loop(0, 9, widen_links, 0)
    sign_rows = (2 * sign[...] - 1).astype(F32)
    sign_rows = jnp.where(tm == n_tm - 1, sign_rows, jnp.ones_like(sign_rows))
    s8[pl.ds(0, 4, stride=2), :] = sign_rows
    s8[pl.ds(1, 4, stride=2), :] = sign_rows
    factor = s8[...]
    for rc in range(9):
        rows = pl.ds((27 + rc) * 32 + 24, 8)
        lf[rows, :] = lf[rows, :] * factor

    ez[...] = jnp.zeros_like(ez)
    hb[:, 0:PAD, :] = jnp.zeros((8, PAD, 128), F32)
    hb[:, PAD + 192 : PAD + 200, :] = jnp.zeros((8, 8, 128), F32)
    rt[:, :, 0:PAD, :] = jnp.zeros((3, 2, PAD, 128), F32)
    rt[:, :, PAD + 48 : PAD + 56, :] = jnp.zeros((3, 2, 8, 128), F32)

    def link(d, r, c, v):
        base = ((d * 9 + r * 3 + c) * 16 + 8 * v) * 2
        return lf[pl.ds(base, 8, stride=2), :], lf[pl.ds(base + 1, 8, stride=2), :]

    def exchange(i, d, forward):
        slot = 2 * d + (0 if forward else 1)
        if d == 3:
            source = st.at[i, slot - 6]
            target = rt.at[i, slot - 6, pl.ds(PAD, 48)]
        else:
            source = sx.at[i, slot]
            target = rx.at[i, slot]
        return pltpu.make_async_remote_copy(
            src_ref=source,
            dst_ref=target,
            send_sem=send_sem.at[i, slot],
            recv_sem=recv_sem.at[i, slot],
            device_id=behind(d) if forward else ahead(d),
            device_id_type=pl.DeviceIdType.MESH,
        )

    def prepare(i, d, read, keep, pack, start=False, ways=(True, False)):
        width = 1 if d == 0 else 8
        which = lx if d == 0 else ly
        faces = {True: [], False: []}
        for v in range(2):
            spin = {}
            for p in range(2):
                for s in range(4):
                    for c in range(3):
                        spin[p, s, c] = read(p, s, c, v)
            half = {True: {}, False: {}}
            for a in range(2):
                source, phase = SPIN[d][a]
                for c in range(3):
                    up = spin[0, a, c], spin[1, a, c]
                    low = spin[0, source, c], spin[1, source, c]
                    half[True][a, c] = add_phase(up, low, NEG[phase])
                    half[False][a, c] = add_phase(up, low, phase)
            carried = {}
            for r in range(3 if False in ways else 0):
                us = [link(d, c, r, v) for c in range(3)]
                for a in range(2):
                    total = None
                    for c in range(3):
                        total = mul_add(total, us[c], half[False][a, c], True)
                    carried[a, r] = total
            half[False] = carried
            for forward in ways:
                slot = 2 * d + (0 if forward else 1)
                for a in range(2):
                    for c in range(3):
                        for p in range(2):
                            j = (a * 3 + c) * 2 + p
                            value = half[forward][a, c][p]
                            if keep:
                                hb[slot, pl.ds(PAD + j * 16 + 8 * v, 8), :] = value
                            faces[forward].append(value)
        if not pack:
            return
        for forward in ways:
            slot = 2 * d + (0 if forward else 1)
            values = faces[forward]
            if d < 2:
                for k in range(3):
                    packed = None
                    for m in range(8):
                        shift = m if forward else m - 7
                        moved = lane_roll(values[8 * k + m], width * shift)
                        packed = moved if packed is None else jnp.where(which == m, moved, packed)
                    sx[i, slot, pl.ds(8 * k, 8), :] = packed
            elif d == 2:
                take = 0 if forward else 3
                for j in range(6):
                    for v in range(2):
                        here, there = values[12 * v + j], lane_roll(values[12 * v + j + 6], 64)
                        pair = (
                            jnp.where(low_half, here, there)
                            if forward
                            else jnp.where(low_half, there, here)
                        )
                        ez[2, pl.ds(j * 16 + 8 * v, 8), :] = pair
                for k in range(3):
                    sx[i, slot, pl.ds(8 * k, 8), :] = ez[2, pl.ds(32 * k + take, 8, stride=4), :]
            else:
                for j in range(12):
                    st[i, slot - 6, pl.ds(4 * j, 4), :] = (
                        values[j][0:4, :] if forward else values[12 + j][4:8, :]
                    )
            if start:
                exchange(i, d, forward).start()

    def send(i, d):
        for forward in (True, False):
            exchange(i, d, forward).start()

    def shifted(i, d, forward, v, part):
        slot = 2 * d + (0 if forward else 1)
        out = []
        if d == 2 and v == 0:
            place = 3 if forward else 0
            for k in range(3):
                ez[1 - int(forward), pl.ds(32 * k + place, 8, stride=4), :] = rx[
                    i, slot, pl.ds(8 * k, 8), :
                ]
        for j in range(12):
            base = PAD + j * 16
            if d < 2:
                width = 1 if d == 0 else 8
                which = lx if d == 0 else ly
                m = v * 12 + j
                local = hb[slot, pl.ds(base + 8 * v, 8), :]
                packed = rx[i, slot, pl.ds(m // 8 * 8, 8), :]
                edge = which == (7 if forward else 0)
                far = near = 0.0
                if part != "local":
                    far = lane_roll(packed, width * (7 - m % 8 if forward else -(m % 8)))
                if part != "remote":
                    near = lane_roll(local, -width if forward else width)
                out.append(jnp.where(edge, far, near))
            elif d == 2:
                local = hb[slot, pl.ds(base + 8 * v, 8), :]
                remote = ez[1 - int(forward), pl.ds(j % 6 * 16 + 8 * v, 8), :]
                if j >= 6:
                    remote = lane_roll(remote, 64)
                if forward:
                    edge = jnp.where(row % 4 == 3, remote, row_roll(local, -1))
                    mixed = jnp.where(low_half, edge, local)
                else:
                    edge = jnp.where(row % 4 == 0, remote, row_roll(local, 1))
                    mixed = jnp.where(low_half, local, edge)
                out.append(lane_roll(mixed, 64))
            elif forward:
                if v == 0:
                    out.append(hb[slot, pl.ds(base + 4, 8), :])
                else:
                    local = hb[slot, pl.ds(base + 12, 8), :]
                    remote = rt[i, 0, pl.ds(PAD + 4 * j - 4, 8), :]
                    out.append(jnp.where(row < 4, local, remote))
            elif v == 1:
                out.append(hb[slot, pl.ds(base + 4, 8), :])
            else:
                local = hb[slot, pl.ds(base - 4, 8), :]
                remote = rt[i, 1, pl.ds(PAD + 4 * j, 8), :]
                out.append(jnp.where(row < 4, remote, local))
        return {(a, c): (out[(a * 3 + c) * 2], out[(a * 3 + c) * 2 + 1]) for a in range(2) for c in range(3)}

    def acc_rows(p, s, c, v):
        return pl.ds(((p * 4 + s) * 3 + c) * 16 + 8 * v, 8)

    def hop(i, d, store, part="both"):
        if part != "local":
            exchange(i, d, True).wait_recv()
            exchange(i, d, False).wait_recv()
        for v in range(2):
            front = shifted(i, d, True, v, part)
            back = shifted(i, d, False, v, part)
            for r in range(3):
                us = [link(d, r, c, v) for c in range(3)]
                for a in range(2):
                    source, phase = SPIN[d][a]
                    w = None
                    for c in range(3):
                        w = mul_add(w, us[c], front[a, c], False)
                    b = back[a, r]
                    upper = acc_ref[acc_rows(0, a, r, v), :], acc_ref[acc_rows(1, a, r, v), :]
                    lower = (
                        acc_ref[acc_rows(0, source, r, v), :],
                        acc_ref[acc_rows(1, source, r, v), :],
                    )
                    upper = upper[0] + (w[0] + b[0]), upper[1] + (w[1] + b[1])
                    lower = add_phase(lower, (b[0] - w[0], b[1] - w[1]), CONJ[phase])
                    store(upper, a, r, v)
                    store(lower, source, r, v)

    def to_acc(value, s, c, v):
        acc_ref[acc_rows(0, s, c, v), :] = value[0]
        acc_ref[acc_rows(1, s, c, v), :] = value[1]

    def clover_term(i):
        for v in range(2):
            for b in range(2):
                x = [
                    tuple(vb[i, spinor_rows(p, 2 * b + n // 3, n % 3, v), :] for p in range(2))
                    for n in range(6)
                ]
                for r in range(6):
                    total = None
                    for n in range(6):
                        base = ((b * 36 + r * 6 + n) * 16 + 8 * v) * 2
                        c = cf[pl.ds(base, 8, stride=2), :], cf[pl.ds(base + 1, 8, stride=2), :]
                        total = mul_add(total, c, x[n], False)
                    s, c = 2 * b + r // 3, r % 3
                    f = tuple(src[spinor_rows(p, s, c, v), :] for p in range(2))
                    to_acc((2.0 * (f[0] - total[0]), 2.0 * (f[1] - total[1])), s, c, v)

    def widen_null(i, carry):
        rows = pl.ds(pl.multiple_of(i * 256, 256), 256)
        nf[rows, :] = null[rows, :].astype(F32)
        return carry

    def current(i):
        return lambda p, s, c, v: vb[i, spinor_rows(p, s, c, v), :]

    def without_y(i):
        return lambda p, s, c, v: vb[i, spinor_rows(p, s, c, v), :] + 0.08 * acc_ref[acc_rows(p, s, c, v), :]

    GROUP = 2

    def restrict(null_ref, res_ref, steps, part, unroll):
        def group(g, carry):
            sums = []
            for n in range(GROUP):
                kv = g * GROUP + n
                total = {}
                for az in range(2):
                    re, im = None, None
                    for c in range(3):
                        for t in range(steps):
                            at = c * 16 * steps + (2 * t + az) * 8
                            half = 48 * steps
                            base = kv * 96 * steps + at
                            n_re = null_ref[pl.ds(pl.multiple_of(base, 8), 8), :]
                            n_im = null_ref[pl.ds(pl.multiple_of(base + half, 8), 8), :]
                            r_re = res_ref[pl.ds(at, 8), :]
                            r_im = res_ref[pl.ds(half + at, 8), :]
                            x = n_re * r_re + n_im * r_im
                            y = n_re * r_im - n_im * r_re
                            re = x if re is None else re + x
                            im = y if im is None else im + y
                    total[0, az], total[1, az] = re, im
                sums += [total[0, 0], total[0, 1], total[1, 0], total[1, 1]]
            for bit in (1, 2, 4):
                first = row // bit % 2 == 0
                sums = [
                    jnp.where(first, x, y) + row_roll(jnp.where(first, y, x), bit)
                    for x, y in zip(sums[0::2], sums[1::2])
                ]
            wsum[part, pl.ds(pl.multiple_of(g * 8, 8), 8), :] = sums[0]
            return carry

        lax.fori_loop(0, NV // GROUP, group, 0, unroll=unroll)

    side = [((lane // 8 - 2 * t) % 8 == 0) | ((lane // 8 - 2 * t) % 8 == 7) for t in range(4)]

    def fold(parts):
        out = parts[0]
        for t in range(1, 4):
            out = jnp.where(side[t], lane_roll(parts[t], 16 * t), out)
        return out

    def fold_null(n, carry):
        for az in range(2):
            parts = [nf[pl.ds(pl.multiple_of(n * 64 + (2 * t + az) * 8, 8), 8), :] for t in range(4)]
            nb[pl.ds(pl.multiple_of(n * 16 + az * 8, 8), 8), :] = fold(parts)
        return carry

    def split(x):
        high = x.astype(BF16)
        return jnp.concatenate([high, (x - high.astype(F32)).astype(BF16)], axis=1)

    def dot_nt(a, b):
        return lax.dot_general(a, b, (((1,), (1,)), ((), ())), preferred_element_type=F32)

    def sums_of(part, member):
        return dot_nt(member, split(wsum[part]))

    lane16 = lax.broadcasted_iota(jnp.int32, (16, 256), 1) % 128
    row16 = lax.broadcasted_iota(jnp.int32, (16, 256), 0)
    inner_member = (lane16 // 32 % 2 * 2 + lane16 // 4 % 2 == row16).astype(F32).astype(BF16)
    outer_member = (lane16 // 8 % 2 * 2 + lane16 // 4 % 2 == row16).astype(F32).astype(BF16)
    spread_lane = lax.broadcasted_iota(jnp.int32, (16, 512), 1)
    spread_row = lax.broadcasted_iota(jnp.int32, (16, 512), 0)
    spread_mask = spread_lane % 256 // 24 % 4 == spread_row

    def inner_layers():
        for p in range(2):
            for s in range(4):
                for c in range(3):
                    for v in range(2):
                        value = 0.5 * acc_ref[acc_rows(p, s, c, v), :]
                        value = jnp.where((ly == 0) | (ly == 7), 0.0, value)
                        rl[spinor_rows(p, s, c, v), :] = value.astype(BF16).astype(F32)
        restrict(nf, rl, 4, 0, 1)
        inner[...] = sums_of(0, inner_member)

    def sweep(i, last):
        clover_term(i)
        hop(i, 1, to_acc, "local")
        hop(i, 3, to_acc)
        hop(i, 0, to_acc)
        hop(i, 2, to_acc)
        if not last:
            for way in (True, False):
                prepare(i + 1, 1, without_y(i), False, True, True, (way,))
        else:
            inner_layers()

        def finish(value, s, c, v):
            for p in range(2):
                rows = spinor_rows(p, s, c, v)
                if last:
                    rl[rows, :] = (0.5 * value[p]).astype(BF16).astype(F32)
                else:
                    vb[i + 1, rows, :] = vb[i, rows, :] + 0.08 * value[p]

        hop(i, 1, finish, "remote")
        if not last:
            for d in (2, 0, 3):
                for way in (False, True):
                    prepare(i + 1, d, current(i + 1), True, True, True, (way,))
            prepare(i + 1, 1, current(i + 1), True, False)

    loads[0].wait()
    for d in (1, 2, 0, 3):
        prepare(0, d, current(0), True, True)
    pl.semaphore_wait(barrier, 8)
    for d in (1, 2, 0, 3):
        send(0, d)

    loads[3].wait()

    def widen_clover(n, carry):
        rows = pl.ds(pl.multiple_of(n * 256, 256), 256)
        cf[rows, :] = clover[rows, :].astype(F32)
        return carry

    lax.fori_loop(0, 9, widen_clover, 0)
    loads[5].wait()
    lax.fori_loop(0, 36, widen_null, 0)
    loads[6].wait()
    for n in range(18):
        of[n] = ops[n].astype(F32)
    out_lane = lax.broadcasted_iota(jnp.int32, (256, 512), 1)
    in_row = lax.broadcasted_iota(jnp.int32, (256, 512), 0) % 128
    q = out_lane % 256 // 24
    match = (
        (in_row // 4 == out_lane % 256 % 24)
        & (in_row // 2 % 2 == out_lane // 256)
        & (in_row % 2 == q // 4)
        & (out_lane % 256 < 192)
        & (in_row < 96)
    )
    gmat[...] = match.astype(F32).astype(BF16)
    wsum[:, 96:128, :] = jnp.zeros((2, 32, 128), F32)
    lax.fori_loop(0, 144, fold_null, 0, unroll=16)
    loads[4].wait()

    def first_sweeps(i, carry):
        sweep(i, False)
        return carry

    lax.fori_loop(0, 2, first_sweeps, 0)
    smooth_ref[...] = vb[2]
    sweep(2, True)

    for n in range(6):
        for az in range(2):
            rb[pl.ds((n * 2 + az) * 8, 8), :] = fold(
                [rl[pl.ds(n * 64 + (2 * t + az) * 8, 8), :] for t in range(4)]
            )
    restrict(nb, rb, 1, 1, 12)
    partial = sums_of(1, outer_member) + inner[...]

    spread = jnp.dot(split(partial), gmat[...], preferred_element_type=F32)
    vector = jnp.sum(jnp.where(spread_mask, spread, 0.0), axis=0, keepdims=True)
    sw[0:1, :] = vector[:, 0:256]
    sw[1:2, :] = vector[:, 256:512]

    def exchange_coarse(d, forward):
        slot = 2 * d + (0 if forward else 1)
        return pltpu.make_async_remote_copy(
            src_ref=sw,
            dst_ref=rw.at[slot],
            send_sem=send_sem.at[3, slot],
            recv_sem=recv_sem.at[3, slot],
            device_id=behind(d) if forward else ahead(d),
            device_id_type=pl.DeviceIdType.MESH,
        )

    order = (1, 0, 2, 3)
    for d in order:
        for forward in (True, False):
            exchange_coarse(d, forward).start()

    lane1 = lax.broadcasted_iota(jnp.int32, (8, 256), 1)
    own = jnp.broadcast_to(sw[0:1, :], (8, 256)), jnp.broadcast_to(sw[1:2, :], (8, 256))

    def apply(total, n, vec):
        w_re, w_im = vec[0][0:1, 0:192], vec[1][0:1, 0:192]
        o_re, o_im = of[2 * n], of[2 * n + 1]
        re = o_re * w_re - o_im * w_im
        im = o_re * w_im + o_im * w_re
        return (re, im) if total is None else (total[0] + re, total[1] + im)

    total = apply(None, 0, own)
    for d in (3, 0, 2, 1):
        for forward in (True, False):
            slot = 2 * d + (0 if forward else 1)
            exchange_coarse(d, forward).wait_recv()
            vec = []
            for p in range(2):
                remote = jnp.broadcast_to(rw[slot, p : p + 1, :], (8, 256))
                if d == 3:
                    vec.append(remote)
                    continue
                step = 1 << d
                near = lane1 // 24 // step % 2 == (0 if forward else 1)
                left = 256 - 24 * step
                right = 24 * step
                if forward:
                    vec.append(jnp.where(near, pltpu.roll(own[p], left, 1), pltpu.roll(remote, right, 1)))
                else:
                    vec.append(jnp.where(near, pltpu.roll(own[p], right, 1), pltpu.roll(remote, left, 1)))
            total = apply(total, 1 + slot, vec)

    seg_lane = lax.broadcasted_iota(jnp.int32, (16, 192), 1)
    segment = (seg_lane // 24 == lax.broadcasted_iota(jnp.int32, (16, 192), 0)).astype(F32).astype(BF16)
    for p in range(2):
        high = total[p].astype(BF16)
        low = (total[p] - high.astype(F32)).astype(BF16)
        result = dot_nt(segment, high) + dot_nt(segment, low)
        coarse_ref[p] = result[0:8, :]

    for d in range(4):
        for forward in (True, False):
            for i in range(3):
                exchange(i, d, forward).wait_send()
            exchange_coarse(d, forward).wait_send()


def hand_on(smooth_in, coarse_in, smooth_out, coarse_out, sem):
    copies = [
        pltpu.make_async_copy(smooth_in, smooth_out, sem.at[0]),
        pltpu.make_async_copy(coarse_in, coarse_out, sem.at[1]),
    ]
    for copy in copies:
        copy.start()
    for copy in copies:
        copy.wait()


def solution(mesh):
    n_space, n_tm = mesh.shape["space"], mesh.shape["tm"]

    def spinor_in(x):
        return x.transpose(0, 2, 1, 3).reshape(6, 4, 16, 128).transpose(0, 2, 1, 3).reshape(384, 128)

    def spinor_out(x):
        return x.reshape(6, 16, 4, 128).transpose(0, 2, 1, 3).reshape(2, 3, 4, 2048).transpose(0, 2, 1, 3)

    def matrix_in(x, count):
        return (
            x.transpose(0, 2, 3, 1, 4)
            .reshape(count, 2, 16, 128)
            .transpose(0, 2, 1, 3)
            .reshape(count * 32, 128)
        )

    def on_device(source_field, initial_guess, gauge_links, clover, boundary_signs, null_vectors, coarse_ops):
        nulls = (
            null_vectors.transpose(0, 1, 3, 2, 4)
            .reshape(144, 4, 16, 128)
            .transpose(0, 2, 1, 3)
            .reshape(9216, 128)
        )
        vmem = pltpu.VMEM
        smoothed, coarse = pl.pallas_call(
            lambda *refs: kernel(n_space, n_tm, *refs),
            out_shape=(
                jax.ShapeDtypeStruct((384, 128), F32),
                jax.ShapeDtypeStruct((2, 8, 24), F32),
            ),
            in_specs=[pl.BlockSpec(memory_space=pl.ANY)] * 7,
            out_specs=(pl.BlockSpec(memory_space=vmem), pl.BlockSpec(memory_space=vmem)),
            scratch_shapes=[
                vmem((384, 128), F32),
                vmem((1152, 128), BF16),
                vmem((2304, 128), BF16),
                vmem((4, 128), jnp.int32),
                vmem((9216, 128), BF16),
                vmem((18, 24, 192), BF16),
                vmem((4, 384, 128), F32),
                vmem((384, 128), F32),
                vmem((1152, 128), F32),
                vmem((2304, 128), F32),
                vmem((9216, 128), F32),
                vmem((18, 24, 192), F32),
                vmem((8, 128), F32),
                vmem((8, 208, 128), F32),
                vmem((384, 128), F32),
                vmem((3, 96, 128), F32),
                vmem((3, 6, 24, 128), F32),
                vmem((3, 2, 48, 128), F32),
                vmem((3, 6, 24, 128), F32),
                vmem((3, 2, 64, 128), F32),
                vmem((2, 128, 128), F32),
                vmem((16, 128), F32),
                vmem((2304, 128), F32),
                vmem((96, 128), F32),
                vmem((2, 256), F32),
                vmem((8, 2, 256), F32),
                vmem((256, 512), BF16),
                pltpu.SemaphoreType.DMA((7,)),
                pltpu.SemaphoreType.DMA((4, 8)),
                pltpu.SemaphoreType.DMA((4, 8)),
            ],
            compiler_params=pltpu.CompilerParams(
                collective_id=0, has_side_effects=True, vmem_limit_bytes=60 * 1024 * 1024
            ),
        )(
            spinor_in(source_field),
            spinor_in(initial_guess),
            matrix_in(gauge_links, 36),
            matrix_in(clover, 72),
            boundary_signs.reshape(4, 128),
            nulls,
            coarse_ops.reshape(18, 24, 192),
        )
        smoothed, coarse = pl.pallas_call(
            hand_on,
            out_shape=(
                jax.ShapeDtypeStruct((384, 128), F32),
                jax.ShapeDtypeStruct((2, 8, 24), F32),
            ),
            in_specs=[pl.BlockSpec(memory_space=vmem)] * 2,
            out_specs=[pl.BlockSpec(memory_space=pl.ANY)] * 2,
            scratch_shapes=[pltpu.SemaphoreType.DMA((2,))],
        )(smoothed, coarse)
        return spinor_out(smoothed), coarse.transpose(0, 2, 1)

    field = P(None, None, None, ("tm", "space"))
    matrix = P(None, None, None, None, ("tm", "space"))
    return jax.shard_map(
        on_device,
        mesh=mesh,
        in_specs=(field, field, matrix, matrix, P("space"), matrix, field),
        out_specs=(field, P(None, None, ("tm", "space"))),
        check_vma=False,
    )
```
